256 devices in a mesh: dom: 16 (over y_lo, z), blk: 16 (over y_hi, x, core).
Axes of the slice: x: 4, y: 4 (y_hi: 2, y_lo: 2; y = y_hi * 2 + y_lo), z: 8, core: 2. Of those that a mesh axis runs over, the one named last changes fastest.
Arguments:
- labels: bfloat16 [524288, 256], P(('dom', 'blk')), may hold values from 0.05 to 12.5
- tags: bfloat16 [524288, 256], P(('dom', 'blk')), may hold values from 0 to 2
- seed_mask: int32 [524288], P(('dom', 'blk')), may hold values 0 or 1
- intra_tiles: bfloat16 [256, 16, 2, 128, 128], P(('dom', 'blk')), may hold values from 3e-05 to 1
- intra_rows: int32 [256, 16, 2], P(('dom', 'blk')), may hold values from 0 to 15, as said below
- intra_cols: int32 [256, 16, 2], P(('dom', 'blk')), may hold values from 0 to 15
- send_list: int32 [256, 16, 1], P(('dom', 'blk')), may hold values from 0 to 15
- cut_tiles: bfloat16 [256, 16, 128, 128], P(('dom', 'blk')), may hold values from 3e-05 to 1
- cut_slot: int32 [256, 16], P(('dom', 'blk')), may hold values from 0 to 15, each once within a row
- cut_rows: int32 [256, 16], P(('dom', 'blk')), may hold values from 0 to 15, as said below
Outputs:
- new_labels: bfloat16 [524288, 256], P(('dom', 'blk'))
The draws below stay inside these ranges and needn't reach their ends.
Inputs may be any that keep to these rules, and one draw needn't show every extreme that they name: `intra_rows`: for each device and panel the 2 entries run cyclically through the row tiles from a drawn offset, so they name distinct row tiles. `cut_slot`: each device names every slot exactly once. `cut_rows`: for each device the 16 entries run cyclically through the row tiles from a drawn offset, so every row tile has cut tiles.
All inputs are finite; a program needn't handle non-finite values. No bound on the sum of `seed_mask` on one device may be relied on, other than what follows from the above.
Results may differ from the reference program's by a relative error of at most 0.001.
Values may be sent and summed in bfloat16 or wider, within the bound.
A program may use at most 128 MiB of HBM per device.

```python
import jax
import jax.numpy as jnp
from jax import lax

D = 256
TILE = 128
TPD = 16
KS = 2
CUTS = 1
KCUT = 16
NODES = 524288
N_DOM = 16
N_BLK = 16
DEVICES = 256


def soft_tags(key, shape, base_spread, hot_share, hot_lowest, hot_highest):
    key_base, key_chooser, key_level = jax.random.split(key, 3)
    base_part = base_spread * jax.random.uniform(key_base, shape, jnp.float32)
    chooser = jax.random.uniform(key_chooser, shape, jnp.float32)
    hot_level = hot_lowest + (hot_highest - hot_lowest) * jax.random.uniform(key_level, shape, jnp.float32)
    return (0.05 + base_part + jnp.where(chooser < hot_share, hot_level, 0.0)).astype(jnp.bfloat16)


def sparse_tiles(key, shape, strong_share, lowest, highest):
    key_base, key_chooser, key_level = jax.random.split(key, 3)
    base_part = lowest * jnp.exp(jnp.log(highest / lowest) * jax.random.uniform(key_base, shape, jnp.float32))
    chooser = jax.random.uniform(key_chooser, shape, jnp.float32)
    strong_part = 0.5 + 0.5 * jax.random.uniform(key_level, shape, jnp.float32)
    return jnp.where(chooser < strong_share, strong_part, base_part).astype(jnp.bfloat16)


def draw_labels(key, part):
    key = jax.random.fold_in(key, 11)
    return soft_tags(key, (NODES, D), 0.25, 0.02, 3.0, 9.0)


def draw_intra_tiles(key, part):
    key = jax.random.fold_in(key, 13)
    return sparse_tiles(key, (DEVICES, N_BLK, KS, TILE, TILE), 1.0 / 64.0, 0.0001, 0.01)


def draw_cut_tiles(key, part):
    key = jax.random.fold_in(key, 17)
    return sparse_tiles(key, (DEVICES, KCUT, TILE, TILE), 1.0 / 64.0, 0.0001, 0.01)


def draw_intra_rows(key, part):
    key = jax.random.fold_in(key, 3)
    offset = jax.random.randint(key, (DEVICES, N_BLK, 1), 0, TPD)
    return ((jnp.arange(KS, dtype=jnp.int32)[None, None, :] + offset) % TPD).astype(jnp.int32)


def draw_cut_rows(key, part):
    key = jax.random.fold_in(key, 7)
    offset = jax.random.randint(key, (DEVICES, 1), 0, TPD)
    return ((jnp.arange(KCUT, dtype=jnp.int32)[None, :] + offset) % TPD).astype(jnp.int32)


def place_ends(values, rng, least, largest):
    index_at = [jax.random.randint(jax.random.fold_in(rng, axis), (), 0, length) for axis, length in enumerate(values.shape)]
    longest = values.shape.index(max(values.shape))
    beside = index_at[:longest] + [(index_at[longest] + 1) % values.shape[longest]] + index_at[longest + 1:]
    return values.at[tuple(index_at)].set(least).at[tuple(beside)].set(largest)


def block_scale(own_key, dims, cuts, low, top_value):
    def one(position, shards_of):
        draws = jax.random.uniform(jax.random.fold_in(jax.random.fold_in(own_key, 6), position), (shards_of,), jnp.float32, low / len(cuts), top_value / len(cuts))
        return jnp.repeat(jnp.exp(draws), dims[position] // shards_of).reshape((-1,) + (1,) * (len(dims) - position - 1))

    level = one(*cuts[0])
    for cut in cuts[1:]:
        level = level * one(*cut)
    return level


def setup_inputs(seed: int = 0) -> dict:
    streams_of = jax.random.split(jax.random.key(seed), 11)
    return {
        "labels": draw_labels(jax.random.fold_in(streams_of[10], 71), 0),
        "tags": jnp.clip(2.0 * jax.random.uniform(streams_of[1], (NODES, D), jnp.float32) ** block_scale(streams_of[1], (NODES, D), ((0, 256),), -0.2, 0.2), 0.0, 2.0).astype(jnp.bfloat16),
        "seed_mask": place_ends((jax.random.randint(streams_of[2], (NODES,), 0, 8) < 1).astype(jnp.int32), jax.random.fold_in(streams_of[2], 1), 0, 1),
        "intra_tiles": draw_intra_tiles(jax.random.fold_in(streams_of[10], 71), 0),
        "intra_rows": draw_intra_rows(jax.random.fold_in(streams_of[10], 71), 0),
        "intra_cols": place_ends(jax.random.randint(streams_of[5], (DEVICES, N_BLK, KS), 0, TPD), jax.random.fold_in(streams_of[5], 1), 0, TPD - 1).astype(jnp.int32),
        "send_list": place_ends(jax.random.randint(streams_of[6], (DEVICES, N_DOM, CUTS), 0, TPD), jax.random.fold_in(streams_of[6], 1), 0, TPD - 1).astype(jnp.int32),
        "cut_tiles": draw_cut_tiles(jax.random.fold_in(streams_of[10], 71), 0),
        "cut_slot": jax.vmap(lambda own: jax.random.permutation(own, KCUT))(jax.random.split(streams_of[8], DEVICES)).reshape((DEVICES, KCUT)).astype(jnp.int32),
        "cut_rows": draw_cut_rows(jax.random.fold_in(streams_of[10], 71), 0),
    }


def reference(labels, tags, seed_mask, intra_tiles, intra_rows, intra_cols, send_list, cut_tiles, cut_slot, cut_rows):
    blocks_all = labels.reshape(-1, TILE, D)

    def device_update(g):
        p = g // N_BLK
        b = g % N_BLK
        weights = intra_tiles[g].astype(jnp.float32)
        columns = (p * N_BLK + jnp.arange(N_BLK, dtype=jnp.int32)[:, None]) * TPD + intra_cols[g]
        blocks = blocks_all[columns].astype(jnp.float32)
        products = jnp.einsum("skab,skbw->skaw", weights, blocks).reshape(-1, TILE, D)
        rows_flat = intra_rows[g].reshape(-1)
        select = (rows_flat[None, :] == jnp.arange(TPD, dtype=jnp.int32)[:, None]).astype(jnp.float32)
        spread = jnp.einsum("tk,kaw->taw", select, products)
        degree = jnp.einsum("tk,ka->ta", select, jnp.sum(weights, axis=-1).reshape(-1, TILE))
        slots = cut_slot[g]
        anchor = slots // CUTS
        which = slots % CUTS
        sender = anchor * N_BLK + b
        cut_columns = sender * TPD + send_list[sender, p, which]
        cut_blocks = blocks_all[cut_columns].astype(jnp.float32)
        cut_weights = cut_tiles[g].astype(jnp.float32)
        cut_select = (cut_rows[g][None, :] == jnp.arange(TPD, dtype=jnp.int32)[:, None]).astype(jnp.float32)
        spread = spread + jnp.einsum("tk,kaw->taw", cut_select, jnp.einsum("kab,kbw->kaw", cut_weights, cut_blocks))
        degree = degree + jnp.einsum("tk,ka->ta", cut_select, jnp.sum(cut_weights, axis=-1))
        prior = lax.dynamic_slice_in_dim(tags, g * (TPD * TILE), TPD * TILE, 0).astype(jnp.float32).reshape(TPD, TILE, D)
        seeded = lax.dynamic_slice_in_dim(seed_mask, g * (TPD * TILE), TPD * TILE, 0).reshape(TPD, TILE, 1)
        mixed = 0.8 * spread / degree[:, :, None] + 0.2 * prior
        return jnp.where(seeded == 1, prior, mixed).astype(jnp.bfloat16)

    result = lax.map(device_update, jnp.arange(DEVICES, dtype=jnp.int32))
    return result.reshape(NODES, D)
```

```python
import functools

import jax
import jax.numpy as jnp
from jax import lax
from jax.experimental import pallas as pl
from jax.experimental.pallas import tpu as pltpu
from jax.sharding import PartitionSpec as P

ALPHA = 0.8
MESH = pl.DeviceIdType.MESH
F32 = jnp.float32
BF16 = jnp.bfloat16
I32 = jnp.int32
TILES = 16
EDGE = 128
WIDTH = 256
GRAIN = 16
GROUP = 8
CHUNKS = (1, 1, 1, 1, 1, 1, 1, 1)
WINDOW = 3


def kernel(
    labels,
    tags,
    seeds,
    intra,
    cut,
    rows_hbm,
    cols_hbm,
    list_hbm,
    slot_hbm,
    crow_hbm,
    out,
    panel,
    prior,
    seedv,
    wi,
    wc,
    irows,
    icols,
    slist,
    cslot,
    crows,
    colmsg,
    listmsg,
    request_land,
    list_land,
    requests,
    partner_list,
    inverse,
    partner_parts,
    mirror_parts,
    x_stage_own,
    x_recv_own,
    x_stage,
    x_recv,
    z_stage_own,
    z_recv_own,
    z_stage,
    z_recv,
    wmt,
    wzt,
    wm,
    wz,
    wzo,
    lanes_m,
    lanes_z,
    lanes_zo,
    scale,
    base,
    total,
    local_sem,
    ask_send,
    ask_recv,
    list_send,
    list_recv,
    hop1_send,
    hop1_recv,
    hop2_send,
    hop2_recv,
    x_send,
    x_got,
    z_send,
    z_got,
):
    chunks = len(CHUNKS)
    starts = [sum(CHUNKS[:c]) for c in range(chunks)]
    dom = lax.axis_index("dom")
    blk = lax.axis_index("blk")
    low, z = dom // GROUP, dom % GROUP
    high, j = blk // GROUP, blk % GROUP
    other_dom = (dom + GROUP) % (2 * GROUP)
    other_blk = (blk + GROUP) % (2 * GROUP)
    partner = (other_dom, blk)
    beyond = (other_dom, other_blk)

    def row_peer(d):
        return (dom, high * GROUP + (j + d) % GROUP)

    def z_peer(d):
        return (low * GROUP + (z + d) % GROUP, blk)

    loads = [
        (cols_hbm, colmsg),
        (list_hbm, listmsg),
        (list_hbm, slist),
        (cols_hbm, icols),
        (labels, panel),
        (rows_hbm, irows),
        (slot_hbm, cslot),
        (crow_hbm, crows),
        (seeds, seedv),
        (cut, wc),
        (intra, wi),
        (tags, prior),
    ]
    loads = [
        pltpu.make_async_copy(src, dst, local_sem.at[i])
        for i, (src, dst) in enumerate(loads)
    ]
    for load in loads:
        load.start()

    barrier = pltpu.get_barrier_semaphore()

    def greet(d, carry):
        pl.semaphore_signal(barrier, inc=1, device_id=row_peer(d), device_id_type=MESH)
        pl.semaphore_signal(barrier, inc=1, device_id=z_peer(d), device_id_type=MESH)
        return carry

    pl.semaphore_signal(barrier, inc=1, device_id=partner, device_id_type=MESH)
    pl.semaphore_signal(barrier, inc=1, device_id=beyond, device_id_type=MESH)
    lax.fori_loop(1, GROUP, greet, 0)
    loads[0].wait()
    loads[1].wait()
    pl.semaphore_wait(barrier, 2 * GROUP)

    def ask(d):
        return pltpu.make_async_remote_copy(
            src_ref=colmsg,
            dst_ref=request_land.at[j],
            send_sem=ask_send.at[d],
            recv_sem=ask_recv.at[d],
            device_id=row_peer(d),
            device_id_type=MESH,
        )

    def ask_arrival(d):
        return pltpu.make_async_remote_copy(
            src_ref=colmsg,
            dst_ref=request_land.at[(j + GROUP - d) % GROUP],
            send_sem=ask_send.at[d],
            recv_sem=ask_recv.at[d],
            device_id=row_peer(d),
            device_id_type=MESH,
        )

    def start_ask(d, carry):
        ask(d).start()
        return carry

    lax.fori_loop(1, GROUP, start_ask, 0)
    tell = pltpu.make_async_remote_copy(
        src_ref=listmsg,
        dst_ref=list_land,
        send_sem=list_send,
        recv_sem=list_recv,
        device_id=partner,
        device_id_type=MESH,
    )
    tell.start()

    hop1 = [
        pltpu.make_async_remote_copy(
            src_ref=labels.at[:, pl.ds(starts[c], CHUNKS[c])],
            dst_ref=partner_parts[c],
            send_sem=hop1_send.at[c],
            recv_sem=hop1_recv.at[c],
            device_id=partner,
            device_id_type=MESH,
        )
        for c in range(chunks)
    ]
    hop2 = [
        pltpu.make_async_remote_copy(
            src_ref=partner_parts[c],
            dst_ref=mirror_parts[c],
            send_sem=hop2_send.at[c],
            recv_sem=hop2_recv.at[c],
            device_id=beyond,
            device_id_type=MESH,
        )
        for c in range(chunks)
    ]
    for c in range(min(WINDOW, chunks)):
        hop1[c].start()

    def spread_order(i):
        return 1 + (i + 3) % (GROUP - 1)

    def z_copy(stage, recv, index, d, slot):
        return pltpu.make_async_remote_copy(
            src_ref=stage.at[d],
            dst_ref=recv.at[slot],
            send_sem=z_send.at[index, d],
            recv_sem=z_got.at[index, d],
            device_id=z_peer(d),
            device_id_type=MESH,
        )

    def x_copy(stage, recv, index, d, slot):
        return pltpu.make_async_remote_copy(
            src_ref=stage.at[d],
            dst_ref=recv.at[slot],
            send_sem=x_send.at[index, d],
            recv_sem=x_got.at[index, d],
            device_id=row_peer(d),
            device_id_type=MESH,
        )

    def z_serve(source, wanted, stage, recv, index):
        def one(i, carry):
            d = spread_order(i)
            stage[d] = source[wanted[0, low * GROUP + (z + d) % GROUP]]
            z_copy(stage, recv, index, d, z).start()
            return carry

        lax.fori_loop(0, GROUP - 1, one, 0)
        recv[z] = source[wanted[0, dom]]

    def x_serve(source, which, stage, recv, index):
        def one(i, carry):
            d = spread_order(i)
            peer = (j + d) % GROUP
            stage[d, 0] = source[requests[peer, 0, which]]
            stage[d, 1] = source[requests[peer, 1, which]]
            x_copy(stage, recv, index, d, j).start()
            return carry

        lax.fori_loop(0, GROUP - 1, one, 0)
        recv[j, 0] = source[icols[0, which]]
        recv[j, 1] = source[icols[1, which]]

    def z_wait(stage, recv, index):
        def one(d, carry):
            z_copy(stage, recv, index, d, (z + GROUP - d) % GROUP).wait_recv()
            return carry

        lax.fori_loop(1, GROUP, one, 0)

    def x_wait(stage, recv, index):
        def one(d, carry):
            x_copy(stage, recv, index, d, (j + GROUP - d) % GROUP).wait_recv()
            return carry

        lax.fori_loop(1, GROUP, one, 0)

    for load in loads[2:5]:
        load.wait()
    z_serve(panel, slist, z_stage_own, z_recv_own, chunks)

    def take_ask(d, carry):
        ask_arrival(d).wait_recv()
        return carry

    lax.fori_loop(1, GROUP, take_ask, 0)
    request_land[j] = colmsg[...]
    settle = pltpu.make_async_copy(request_land, requests, local_sem.at[0])
    settle.start()
    settle.wait()
    x_serve(panel, blk, x_stage_own, x_recv_own, chunks)

    def lane_index(width):
        return lax.broadcasted_iota(I32, (GRAIN, width), 1)

    def prepare_cut():
        for load in loads[5:10]:
            load.wait()

        def invert(q, carry):
            found = jnp.int32(0)
            for k in range(TILES):
                found = jnp.where(cslot[0, k] == q, k, found)
            inverse[q] = found
            return carry

        lax.fori_loop(0, TILES, invert, 0)
        lane = lane_index(WIDTH)
        for b in range(GROUP // 2):
            k0 = inverse[low * GROUP + 2 * b]
            k1 = inverse[low * GROUP + 2 * b + 1]
            wzo[b, :, 0:EDGE] = wc[k0]
            wzo[b, :, EDGE : 2 * EDGE] = wc[k1]
            lanes_zo[b] = jnp.where(lane < EDGE, crows[0, k0], crows[0, k1])
        lane = lane_index(GROUP * GRAIN) // GRAIN
        ids = jnp.zeros((GRAIN, GROUP * GRAIN), I32)
        for q in range(GROUP):
            ids = jnp.where(lane == q, crows[0, inverse[(1 - low) * GROUP + q]], ids)
        lanes_z[...] = ids

        def turn(q, carry):
            flipped = wc[inverse[(1 - low) * GROUP + q]].T
            for c in range(TILES // 2):
                wzt[c, pl.ds(pl.multiple_of(q * GRAIN, GRAIN), GRAIN), :] = flipped[
                    c * GRAIN : (c + 1) * GRAIN, :
                ]
            return carry

        lax.fori_loop(0, GROUP, turn, 0)

        def back(c, carry):
            wz[c] = wzt[c].T
            return carry

        lax.fori_loop(0, TILES // 2, back, 0)

    def prepare_mirror():
        loads[10].wait()
        lane = lane_index(2 * GROUP * GRAIN) // GRAIN
        ids = jnp.zeros((GRAIN, 2 * GROUP * GRAIN), I32)
        for p in range(GROUP):
            for k in range(2):
                ids = jnp.where(
                    lane == 2 * p + k, irows[k, (1 - high) * GROUP + p], ids
                )
        lanes_m[...] = ids

        def turn(p, carry):
            for k in range(2):
                flipped = wi[(1 - high) * GROUP + p, k].T
                for c in range(TILES // 2):
                    wmt[
                        c,
                        pl.ds(pl.multiple_of((2 * p + k) * GRAIN, GRAIN), GRAIN),
                        :,
                    ] = flipped[c * GRAIN : (c + 1) * GRAIN, :]
            return carry

        lax.fori_loop(0, GROUP, turn, 0)

        def back(c, carry):
            wm[c, :, 0:EDGE] = wmt[c, 0:EDGE, :].T
            wm[c, :, EDGE : 2 * EDGE] = wmt[c, EDGE : 2 * EDGE, :].T
            return carry

        lax.fori_loop(0, TILES // 2, back, 0)

    def prepare_scale():
        tile = lax.broadcasted_iota(I32, (EDGE, 2 * EDGE), 0)
        lane = lax.broadcasted_iota(I32, (EDGE, 2 * EDGE), 1)

        def sums(weights, row0, row1):
            chosen = jnp.where(tile == jnp.where(lane < EDGE, row0, row1), 1.0, 0.0)
            return lax.dot_general(
                weights,
                chosen.astype(BF16),
                (((1,), (1,)), ((), ())),
                preferred_element_type=F32,
            )

        def intra_sums(s, degree):
            weights = jnp.concatenate([wi[s, 0], wi[s, 1]], axis=1)
            return degree + sums(weights, irows[0, s], irows[1, s])

        def cut_sums(h, degree):
            weights = jnp.concatenate([wc[2 * h], wc[2 * h + 1]], axis=1)
            return degree + sums(weights, crows[0, 2 * h], crows[0, 2 * h + 1])

        degree = lax.fori_loop(0, TILES, intra_sums, jnp.zeros((EDGE, EDGE), F32))
        degree = lax.fori_loop(0, TILES // 2, cut_sums, degree)
        used = lax.broadcasted_iota(I32, (EDGE, EDGE), 1) < TILES
        mask = jnp.concatenate(
            [seedv[...].astype(F32), jnp.zeros((EDGE - TILES, EDGE), F32)], axis=0
        ).T
        factor = jnp.where(mask > 0.5, 0.0, ALPHA / jnp.where(used, degree, 1.0))
        rest = jnp.where(mask > 0.5, 1.0, 1.0 - ALPHA)
        loads[11].wait()
        for t in range(TILES):
            scale[t] = jnp.broadcast_to(factor[:, t : t + 1], (EDGE, EDGE))
            share = jnp.broadcast_to(rest[:, t : t + 1], (EDGE, EDGE))
            share = jnp.concatenate([share, share], axis=1)
            base[t] = prior[t].astype(F32) * share

    span = 4

    def spread_part(tg, blocks):
        part = None
        for weights, ids, values in blocks:
            pieces = []
            width = weights.shape[1]
            cube = weights.reshape(EDGE // GRAIN, GRAIN, width)
            for u in range(span):
                keep = jnp.where(ids == tg * span + u, 1.0, 0.0).astype(BF16)
                pieces.append((cube * keep[None]).reshape(EDGE, width))
            lhs = jnp.concatenate(pieces, axis=0)
            term = jnp.dot(lhs, values, preferred_element_type=F32)
            part = term if part is None else part + term
        return part

    def gather_own_x(first, count):
        def one(tg, carry):
            lane = lane_index(WIDTH)
            blocks = []
            for p in range(first, first + count):
                s = high * GROUP + p
                ids = jnp.where(lane < EDGE, irows[0, s], irows[1, s])
                weights = jnp.concatenate([wi[s, 0], wi[s, 1]], axis=1)
                values = x_recv_own[p].reshape(2 * EDGE, WIDTH)
                blocks.append((weights, ids, values))
            at = pl.ds(pl.multiple_of(tg * span * EDGE, EDGE), span * EDGE)
            total[at, :] += spread_part(tg, blocks)
            return carry

        lax.fori_loop(0, TILES // span, one, 0)

    def gather_own_z():
        z_wait(z_stage_own, z_recv_own, chunks)

        def one(tg, carry):
            blocks = []
            for b in range(GROUP // 2):
                values = z_recv_own[2 * b : 2 * b + 2].reshape(2 * EDGE, WIDTH)
                blocks.append((wzo[b], lanes_zo[b], values))
            at = pl.ds(pl.multiple_of(tg * span * EDGE, EDGE), span * EDGE)
            total[at, :] = spread_part(tg, blocks)
            return carry

        lax.fori_loop(0, TILES // span, one, 0)

    def chunk_blocks(c):
        return [
            (wm[c], lanes_m[...], x_recv[c][...].reshape(2 * GROUP * GRAIN, WIDTH)),
            (wz[c], lanes_z[...], z_recv[c][...].reshape(GROUP * GRAIN, WIDTH)),
        ]

    def gather_chunks(cs):
        for c in cs:
            z_wait(z_stage[c], z_recv[c], c)
            x_wait(x_stage[c], x_recv[c], c)

        def one(tg, carry):
            blocks = []
            for c in cs:
                blocks += chunk_blocks(c)
            at = pl.ds(pl.multiple_of(tg * span * EDGE, EDGE), span * EDGE)
            total[at, :] += spread_part(tg, blocks)
            return carry

        lax.fori_loop(0, TILES // span, one, 0)

    def finish(c):
        z_wait(z_stage[c], z_recv[c], c)
        x_wait(x_stage[c], x_recv[c], c)

        def one(tg, carry):
            at = pl.ds(pl.multiple_of(tg * span * EDGE, EDGE), span * EDGE)
            spread = total[at, :] + spread_part(tg, chunk_blocks(c))
            factor = scale[pl.ds(tg * span, span)].reshape(span * EDGE, EDGE)
            factor = jnp.concatenate([factor, factor], axis=1)
            rest = base[pl.ds(tg * span, span)].reshape(span * EDGE, WIDTH)
            out[at, :] = (factor * spread + rest).astype(BF16)
            return carry

        lax.fori_loop(0, TILES // span, one, 0)

    def own_x_first():
        x_wait(x_stage_own, x_recv_own, chunks)
        gather_own_x(0, 4)

    work = {
        0: [prepare_cut],
        1: [prepare_mirror],
        2: [prepare_scale],
        3: [],
        4: [gather_own_z],
        5: [own_x_first],
        6: [lambda: gather_own_x(4, 4)],
        7: [lambda: gather_chunks([0, 1, 2, 3])],
        8: [lambda: gather_chunks([4, 5]), lambda: gather_chunks([6])],
    }
    for c in range(chunks + 1):
        if c < chunks:
            hop1[c].wait_recv()
            hop2[c].start()
            if c + WINDOW < chunks:
                hop1[c].wait_send()
                hop1[c + WINDOW].start()
            if c == 0:
                tell.wait_recv()
                settle = pltpu.make_async_copy(list_land, partner_list, local_sem.at[0])
                settle.start()
                settle.wait()
            z_serve(partner_parts[c], partner_list, z_stage[c], z_recv[c], c)
        if c >= 1:
            hop2[c - 1].wait_recv()
            x_serve(mirror_parts[c - 1], other_blk, x_stage[c - 1], x_recv[c - 1], c - 1)
        for piece in work[c]:
            piece()
    finish(chunks - 1)

    def left(d, carry):
        ask(d).wait_send()
        z_copy(z_stage_own, z_recv_own, chunks, d, z).wait_send()
        x_copy(x_stage_own, x_recv_own, chunks, d, j).wait_send()
        for c in range(chunks):
            z_copy(z_stage[c], z_recv[c], c, d, z).wait_send()
            x_copy(x_stage[c], x_recv[c], c, d, j).wait_send()
        return carry

    lax.fori_loop(1, GROUP, left, 0)
    tell.wait_send()
    for c in range(chunks):
        if c + WINDOW >= chunks:
            hop1[c].wait_send()
        hop2[c].wait_send()


def on_device(
    labels,
    tags,
    seed_mask,
    intra_tiles,
    intra_rows,
    intra_cols,
    send_list,
    cut_tiles,
    cut_slot,
    cut_rows,
):
    chunks = len(CHUNKS)

    def flat(ids):
        return jnp.swapaxes(ids[0], 0, 1)

    parts = EDGE // GRAIN
    operands = (
        labels.reshape(TILES, parts, GRAIN, WIDTH),
        tags.reshape(TILES, EDGE, WIDTH),
        seed_mask.reshape(TILES, EDGE),
        intra_tiles.reshape(TILES, 2, EDGE, EDGE),
        cut_tiles.reshape(TILES, EDGE, EDGE),
        flat(intra_rows),
        flat(intra_cols),
        flat(send_list),
        cut_slot,
        cut_rows,
    )
    vmem = pltpu.VMEM
    smem = pltpu.SMEM

    def per_chunk(*shape):
        return [
            vmem(tuple(g if n is None else n for n in shape), BF16) for g in CHUNKS
        ]

    scratch = [
        vmem((TILES, parts, GRAIN, WIDTH), BF16),
        vmem((TILES, EDGE, WIDTH), BF16),
        vmem((TILES, EDGE), I32),
        vmem((TILES, 2, EDGE, EDGE), BF16),
        vmem((TILES, EDGE, EDGE), BF16),
        smem((2, TILES), I32),
        smem((2, TILES), I32),
        smem((1, TILES), I32),
        smem((1, TILES), I32),
        smem((1, TILES), I32),
        vmem((2, TILES), I32),
        vmem((1, TILES), I32),
        vmem((GROUP, 2, TILES), I32),
        vmem((1, TILES), I32),
        smem((GROUP, 2, TILES), I32),
        smem((1, TILES), I32),
        smem((TILES,), I32),
        per_chunk(TILES, None, GRAIN, WIDTH),
        per_chunk(TILES, None, GRAIN, WIDTH),
        vmem((GROUP, 2, parts, GRAIN, WIDTH), BF16),
        vmem((GROUP, 2, parts, GRAIN, WIDTH), BF16),
        per_chunk(GROUP, 2, None, GRAIN, WIDTH),
        per_chunk(GROUP, 2, None, GRAIN, WIDTH),
        vmem((GROUP, parts, GRAIN, WIDTH), BF16),
        vmem((GROUP, parts, GRAIN, WIDTH), BF16),
        per_chunk(GROUP, None, GRAIN, WIDTH),
        per_chunk(GROUP, None, GRAIN, WIDTH),
        vmem((parts, 2 * GROUP * GRAIN, EDGE), BF16),
        vmem((parts, GROUP * GRAIN, EDGE), BF16),
        vmem((parts, EDGE, 2 * GROUP * GRAIN), BF16),
        vmem((parts, EDGE, GROUP * GRAIN), BF16),
        vmem((GROUP // 2, EDGE, 2 * EDGE), BF16),
        vmem((GRAIN, 2 * GROUP * GRAIN), I32),
        vmem((GRAIN, GROUP * GRAIN), I32),
        vmem((GROUP // 2, GRAIN, 2 * EDGE), I32),
        vmem((TILES, EDGE, EDGE), F32),
        vmem((TILES, EDGE, WIDTH), F32),
        vmem((TILES * EDGE, WIDTH), F32),
        pltpu.SemaphoreType.DMA((12,)),
        pltpu.SemaphoreType.DMA((GROUP,)),
        pltpu.SemaphoreType.DMA((GROUP,)),
        pltpu.SemaphoreType.DMA,
        pltpu.SemaphoreType.DMA,
        pltpu.SemaphoreType.DMA((chunks,)),
        pltpu.SemaphoreType.DMA((chunks,)),
        pltpu.SemaphoreType.DMA((chunks,)),
        pltpu.SemaphoreType.DMA((chunks,)),
        pltpu.SemaphoreType.DMA((chunks + 1, GROUP)),
        pltpu.SemaphoreType.DMA((chunks + 1, GROUP)),
        pltpu.SemaphoreType.DMA((chunks + 1, GROUP)),
        pltpu.SemaphoreType.DMA((chunks + 1, GROUP)),
    ]
    return pl.pallas_call(
        kernel,
        out_shape=jax.ShapeDtypeStruct((TILES * EDGE, WIDTH), BF16),
        in_specs=[pl.BlockSpec(memory_space=pl.ANY)] * len(operands),
        out_specs=pl.BlockSpec(memory_space=pltpu.VMEM),
        scratch_shapes=scratch,
        compiler_params=pltpu.CompilerParams(
            collective_id=0, has_side_effects=True, vmem_limit_bytes=62 * 2**20
        ),
        name="propagate",
    )(*operands)


def solution(mesh):
    both = ("dom", "blk")
    placed = (
        P(both, None),
        P(both, None),
        P(both),
        P(both, None, None, None, None),
        P(both, None, None),
        P(both, None, None),
        P(both, None, None),
        P(both, None, None, None),
        P(both, None),
        P(both, None),
    )
    return jax.shard_map(
        on_device, mesh=mesh, in_specs=placed, out_specs=P(both, None), check_vma=False
    )
```

```python
import jax
import jax.numpy as jnp
from jax import lax
from jax.experimental import pallas as pl
from jax.experimental.pallas import tpu as pltpu
from jax.sharding import PartitionSpec as P

ALPHA = 0.8
MESH = pl.DeviceIdType.MESH
F32 = jnp.float32
BF16 = jnp.bfloat16
I32 = jnp.int32
TILES = 16
EDGE = 128
WIDTH = 256
GRAIN = 16
PARTS = EDGE // GRAIN
GROUP = 8
SPAN = 4
CHUNKS = (1, 1, 1, 1, 1, 1, 1, 1)


def kernel(
    labels,
    tags,
    seeds,
    intra,
    cut,
    rows_hbm,
    cols_hbm,
    list_hbm,
    slot_hbm,
    crow_hbm,
    out,
    panel,
    prior,
    seedv,
    wi,
    wc,
    irows,
    icols,
    slist,
    cslot,
    crows,
    colmsg,
    listmsg,
    request_land,
    list_land,
    requests,
    partner_list,
    partner_parts,
    mirror_parts,
    x_stage_own,
    x_recv_own,
    x_stage,
    x_recv,
    z_stage_own,
    z_stage,
    z_recv,
    wmt,
    wm,
    lanes_m,
    degree,
    scale,
    base,
    total,
    local_sem,
    ask_send,
    ask_recv,
    list_send,
    list_recv,
    hop1_send,
    hop1_recv,
    hop2_send,
    hop2_recv,
    x_send,
    x_got,
    z_send,
    z_got,
):
    chunks = len(CHUNKS)
    own = chunks
    starts = [sum(CHUNKS[:c]) for c in range(chunks)]
    dom = lax.axis_index("dom")
    blk = lax.axis_index("blk")
    low, z = dom // GROUP, dom % GROUP
    high, j = blk // GROUP, blk % GROUP
    other_dom = (dom + GROUP) % (2 * GROUP)
    other_blk = (blk + GROUP) % (2 * GROUP)
    partner = (other_dom, blk)
    beyond = (other_dom, other_blk)

    def row_peer(d):
        return (dom, high * GROUP + (j + d) % GROUP)

    def z_peer(d):
        return (low * GROUP + (z + d) % GROUP, blk)

    def remote(src, dst, send, recv, device):
        return pltpu.make_async_remote_copy(
            src_ref=src,
            dst_ref=dst,
            send_sem=send,
            recv_sem=recv,
            device_id=device,
            device_id_type=MESH,
        )

    loads = [
        (cols_hbm, colmsg),
        (list_hbm, listmsg),
        (list_hbm, slist),
        (labels, panel),
        (cols_hbm, icols),
        (rows_hbm, irows),
        (intra, wi),
        (slot_hbm, cslot),
        (crow_hbm, crows),
        (seeds, seedv),
        (cut, wc),
        (tags, prior),
    ]
    loads = [
        pltpu.make_async_copy(src, dst, local_sem.at[i])
        for i, (src, dst) in enumerate(loads)
    ]

    barrier = pltpu.get_barrier_semaphore()

    def greet(d, carry):
        pl.semaphore_signal(barrier, inc=1, device_id=row_peer(d), device_id_type=MESH)
        pl.semaphore_signal(barrier, inc=1, device_id=z_peer(d), device_id_type=MESH)
        return carry

    pl.semaphore_signal(barrier, inc=1, device_id=partner, device_id_type=MESH)
    pl.semaphore_signal(barrier, inc=1, device_id=beyond, device_id_type=MESH)
    lax.fori_loop(1, GROUP, greet, 0)
    for load in loads:
        load.start()
    for load in loads[0:3]:
        load.wait()
    pl.semaphore_wait(barrier, 2 * GROUP)

    def ask(d):
        return remote(
            colmsg, request_land.at[d], ask_send.at[d], ask_recv.at[d], row_peer(d)
        )

    def start_ask(d, carry):
        ask(d).start()
        return carry

    lax.fori_loop(1, GROUP, start_ask, 0)
    tell = remote(listmsg, list_land, list_send, list_recv, partner)
    tell.start()

    hop1 = [
        remote(
            labels.at[:, pl.ds(starts[c], CHUNKS[c])],
            partner_parts[c],
            hop1_send.at[c],
            hop1_recv.at[c],
            partner,
        )
        for c in range(chunks)
    ]
    hop2 = [
        remote(
            partner_parts[c],
            mirror_parts[c],
            hop2_send.at[c],
            hop2_recv.at[c],
            beyond,
        )
        for c in range(chunks)
    ]
    for c in range(chunks):
        hop1[c].start()

    others = pl.ds(1, GROUP - 1)

    def spread_order(i):
        return 1 + (i + 3) % (GROUP - 1)

    def z_refs(index, at):
        if index == own:
            return z_stage_own.at[at], z_recv.at[0, at]
        rows = pl.ds(starts[index], CHUNKS[index])
        return z_stage[index].at[at], z_recv.at[1, at, rows]

    def x_refs(index, at):
        if index == own:
            return x_stage_own.at[at], x_recv_own.at[at]
        return x_stage[index].at[at], x_recv[index].at[at]

    def z_copy(index, at, d):
        src, dst = z_refs(index, at)
        return remote(src, dst, z_send.at[index], z_got.at[index], z_peer(d))

    def x_copy(index, at, d):
        src, dst = x_refs(index, at)
        return remote(src, dst, x_send.at[index], x_got.at[index], row_peer(d))

    def z_serve(source, wanted, index):
        stage = z_stage_own if index == own else z_stage[index]

        def one(i, carry):
            d = spread_order(i)
            stage[d] = source[wanted[0, low * GROUP + (z + d) % GROUP]]
            z_copy(index, d, d).start()
            return carry

        lax.fori_loop(0, GROUP - 1, one, 0)
        mine = source[wanted[0, dom]]
        if index == own:
            z_recv[0, 0] = mine
        else:
            z_recv[1, 0, starts[index] : starts[index] + CHUNKS[index]] = mine

    def x_serve(source, which, index):
        stage, recv = (
            (x_stage_own, x_recv_own)
            if index == own
            else (x_stage[index], x_recv[index])
        )

        def one(i, carry):
            d = spread_order(i)
            stage[d, 0] = source[requests[GROUP - d, 0, which]]
            stage[d, 1] = source[requests[GROUP - d, 1, which]]
            x_copy(index, d, d).start()
            return carry

        lax.fori_loop(0, GROUP - 1, one, 0)
        recv[0, 0] = source[icols[0, which]]
        recv[0, 1] = source[icols[1, which]]

    def z_wait(index):
        z_copy(index, others, 1).wait_recv()

    def x_wait(index):
        x_copy(index, others, 1).wait_recv()

    loads[3].wait()
    z_serve(panel, slist, own)

    def take_ask(d, carry):
        ask(d).wait_recv()
        return carry

    lax.fori_loop(1, GROUP, take_ask, 0)
    settle = pltpu.make_async_copy(request_land, requests, local_sem.at[0])
    settle.start()
    loads[4].wait()
    settle.wait()
    x_serve(panel, blk, own)

    lane = lax.broadcasted_iota(I32, (GRAIN, 2 * EDGE), 1)

    def sender(d):
        return (j + GROUP - d) % GROUP

    def mirror_ids():
        loads[5].wait()
        loads[6].wait()
        slot = lane // GRAIN
        ids = jnp.zeros((GRAIN, 2 * EDGE), I32)
        for d in range(GROUP):
            for k in range(2):
                row = irows[k, (1 - high) * GROUP + sender(d)]
                ids = jnp.where(slot == 2 * d + k, row, ids)
        lanes_m[...] = ids

    def mirror_turn(first, count):
        def turn(d, carry):
            for k in range(2):
                flipped = wi[(1 - high) * GROUP + sender(d), k].T
                at = pl.ds(pl.multiple_of((2 * d + k) * GRAIN, GRAIN), GRAIN)
                for c in range(PARTS):
                    wmt[c, at, :] = flipped[c * GRAIN : (c + 1) * GRAIN, :]
            return carry

        lax.fori_loop(first, first + count, turn, 0)

    def mirror_back(first, count):
        def back(c, carry):
            wm[c, :, 0:EDGE] = wmt[c, 0:EDGE, :].T
            wm[c, :, EDGE : 2 * EDGE] = wmt[c, EDGE : 2 * EDGE, :].T
            return carry

        lax.fori_loop(first, first + count, back, 0)

    def sums(weights, row0, row1):
        tile = lax.broadcasted_iota(I32, (EDGE, 2 * EDGE), 0)
        wide = lax.broadcasted_iota(I32, (EDGE, 2 * EDGE), 1)
        chosen = jnp.where(tile == jnp.where(wide < EDGE, row0, row1), 1.0, 0.0)
        return lax.dot_general(
            weights,
            chosen.astype(BF16),
            (((1,), (1,)), ((), ())),
            preferred_element_type=F32,
        )

    def intra_degree(first, count):
        def one(s, value):
            weights = jnp.concatenate([wi[s, 0], wi[s, 1]], axis=1)
            return value + sums(weights, irows[0, s], irows[1, s])

        start = degree[...] if first else jnp.zeros((EDGE, EDGE), F32)
        degree[...] = lax.fori_loop(first, first + count, one, start)

    def cut_degree():
        for load in loads[7:12]:
            load.wait()

        def one(h, value):
            weights = jnp.concatenate([wc[2 * h], wc[2 * h + 1]], axis=1)
            return value + sums(weights, crows[0, 2 * h], crows[0, 2 * h + 1])

        degree[...] = lax.fori_loop(0, TILES // 2, one, degree[...])

    def set_scale(first, count):
        used = lax.broadcasted_iota(I32, (EDGE, EDGE), 1) < TILES
        mask = jnp.concatenate(
            [seedv[...].astype(F32), jnp.zeros((EDGE - TILES, EDGE), F32)], axis=0
        ).T
        factor = jnp.where(mask > 0.5, 0.0, ALPHA / jnp.where(used, degree[...], 1.0))
        rest = jnp.where(mask > 0.5, 1.0, 1.0 - ALPHA)
        for t in range(first, first + count):
            scale[t] = jnp.broadcast_to(factor[:, t : t + 1], (EDGE, EDGE))
            share = jnp.broadcast_to(rest[:, t : t + 1], (EDGE, EDGE))
            share = jnp.concatenate([share, share], axis=1)
            base[t] = prior[t].astype(F32) * share

    def spread_part(tg, blocks):
        part = None
        for weights, ids, values in blocks:
            pieces = []
            width = weights.shape[1]
            cube = weights.reshape(PARTS, GRAIN, width)
            for u in range(SPAN):
                keep = jnp.where(ids == tg * SPAN + u, 1.0, 0.0).astype(BF16)
                pieces.append((cube * keep[None]).reshape(EDGE, width))
            lhs = jnp.concatenate(pieces, axis=0)
            term = jnp.dot(lhs, values, preferred_element_type=F32)
            part = term if part is None else part + term
        return part

    def row_span(tg):
        return pl.ds(pl.multiple_of(tg * SPAN * EDGE, EDGE), SPAN * EDGE)

    def own_x(first, count, lo, hi):
        def one(tg, carry):
            blocks = []
            for d in range(first, first + count):
                s = high * GROUP + sender(d)
                ids = jnp.where(lane < EDGE, irows[0, s], irows[1, s])
                weights = jnp.concatenate([wi[s, 0], wi[s, 1]], axis=1)
                values = x_recv_own[d].reshape(2 * EDGE, WIDTH)
                blocks.append((weights, ids, values))
            part = spread_part(tg, blocks)
            if first == 0:
                total[row_span(tg), :] = part
            else:
                total[row_span(tg), :] += part
            return carry

        lax.fori_loop(lo, hi, one, 0)

    def chunk_blocks(c):
        return [
            (
                wm[starts[c] + g],
                lanes_m[...],
                x_recv[c][:, :, g].reshape(2 * EDGE, WIDTH),
            )
            for g in range(CHUNKS[c])
        ]

    def mirror_x(cs):
        def one(tg, carry):
            blocks = []
            for c in cs:
                blocks += chunk_blocks(c)
            total[row_span(tg), :] += spread_part(tg, blocks)
            return carry

        lax.fori_loop(0, TILES // SPAN, one, 0)

    def add_cut():
        def one(t, carry):
            k = (t + TILES - crows[0, 0]) % TILES
            q = cslot[0, k]
            group = jnp.where(q // GROUP == low, 0, 1)
            block = z_recv[group, (z + GROUP - q % GROUP) % GROUP]
            at = pl.ds(pl.multiple_of(t * EDGE, EDGE), EDGE)
            total[at, :] += jnp.dot(
                wc[k], block.reshape(EDGE, WIDTH), preferred_element_type=F32
            )
            return carry

        lax.fori_loop(0, TILES, one, 0, unroll=2)

    def finish(c):
        def one(tg, carry):
            at = row_span(tg)
            spread = total[at, :] + spread_part(tg, chunk_blocks(c))
            factor = scale[pl.ds(tg * SPAN, SPAN)].reshape(SPAN * EDGE, EDGE)
            factor = jnp.concatenate([factor, factor], axis=1)
            rest = base[pl.ds(tg * SPAN, SPAN)].reshape(SPAN * EDGE, WIDTH)
            out[at, :] = (factor * spread + rest).astype(BF16)
            return carry

        lax.fori_loop(0, TILES // SPAN, one, 0)

    def many(*pieces):
        def run():
            for piece in pieces:
                piece()

        return run

    work = [
        [(mirror_ids,), (mirror_turn, 0, 4)],
        [(mirror_turn, 4, 4), (mirror_back, 0, 4)],
        [(mirror_back, 4, 4), (intra_degree, 0, 16)],
        [(cut_degree,), (set_scale, 0, 4)],
        [(set_scale, 4, 12)],
        [(x_wait, own), (own_x, 0, 4, 0, 4)],
        [(own_x, 4, 4, 0, 4)],
        [(x_wait, 0), (x_wait, 1), (x_wait, 2), (x_wait, 3), (mirror_x, [0, 1, 2, 3])],
        [(x_wait, 4), (x_wait, 5), (mirror_x, [4, 5]), (x_wait, 6), (mirror_x, [6])],
    ]
    for c in range(chunks + 1):
        if c < chunks:
            hop1[c].wait_recv()
            hop2[c].start()
            if c == 0:
                tell.wait_recv()
                settle = pltpu.make_async_copy(list_land, partner_list, local_sem.at[1])
                settle.start()
                settle.wait()
            z_serve(partner_parts[c], partner_list, c)
        if c >= 1:
            hop2[c - 1].wait_recv()
            x_serve(mirror_parts[c - 1], other_blk, c - 1)
        for piece, *given in work[c]:
            piece(*given)
    z_wait(own)
    for c in range(chunks):
        z_wait(c)
    add_cut()
    x_wait(chunks - 1)
    finish(chunks - 1)

    def left(d, carry):
        ask(d).wait_send()
        return carry

    lax.fori_loop(1, GROUP, left, 0)
    tell.wait_send()
    for c in range(chunks + 1):
        z_copy(c, others, 1).wait_send()
        x_copy(c, others, 1).wait_send()
    for c in range(chunks):
        hop1[c].wait_send()
        hop2[c].wait_send()


def on_device(
    labels,
    tags,
    seed_mask,
    intra_tiles,
    intra_rows,
    intra_cols,
    send_list,
    cut_tiles,
    cut_slot,
    cut_rows,
):
    chunks = len(CHUNKS)

    def flat(ids):
        return jnp.swapaxes(ids[0], 0, 1)

    operands = (
        labels.reshape(TILES, PARTS, GRAIN, WIDTH),
        tags.reshape(TILES, EDGE, WIDTH),
        seed_mask.reshape(TILES, EDGE),
        intra_tiles.reshape(TILES, 2, EDGE, EDGE),
        cut_tiles.reshape(TILES, EDGE, EDGE),
        flat(intra_rows),
        flat(intra_cols),
        flat(send_list),
        cut_slot,
        cut_rows,
    )
    operands = [pltpu.with_memory_space_constraint(x, pltpu.HBM) for x in operands]
    vmem = pltpu.VMEM
    smem = pltpu.SMEM
    dma = pltpu.SemaphoreType.DMA

    def per_chunk(*shape):
        return [
            vmem(tuple(g if n is None else n for n in shape), BF16) for g in CHUNKS
        ]

    scratch = [
        vmem((TILES, PARTS, GRAIN, WIDTH), BF16),
        vmem((TILES, EDGE, WIDTH), BF16),
        vmem((TILES, EDGE), I32),
        vmem((TILES, 2, EDGE, EDGE), BF16),
        vmem((TILES, EDGE, EDGE), BF16),
        smem((2, TILES), I32),
        smem((2, TILES), I32),
        smem((1, TILES), I32),
        smem((1, TILES), I32),
        smem((1, TILES), I32),
        vmem((2, TILES), I32),
        vmem((1, TILES), I32),
        vmem((GROUP, 2, TILES), I32),
        vmem((1, TILES), I32),
        smem((GROUP, 2, TILES), I32),
        smem((1, TILES), I32),
        per_chunk(TILES, None, GRAIN, WIDTH),
        per_chunk(TILES, None, GRAIN, WIDTH),
        vmem((GROUP, 2, PARTS, GRAIN, WIDTH), BF16),
        vmem((GROUP, 2, PARTS, GRAIN, WIDTH), BF16),
        per_chunk(GROUP, 2, None, GRAIN, WIDTH),
        per_chunk(GROUP, 2, None, GRAIN, WIDTH),
        vmem((GROUP, PARTS, GRAIN, WIDTH), BF16),
        per_chunk(GROUP, None, GRAIN, WIDTH),
        vmem((2, GROUP, PARTS, GRAIN, WIDTH), BF16),
        vmem((PARTS, 2 * EDGE, EDGE), BF16),
        vmem((PARTS, EDGE, 2 * EDGE), BF16),
        vmem((GRAIN, 2 * EDGE), I32),
        vmem((EDGE, EDGE), F32),
        vmem((TILES, EDGE, EDGE), F32),
        vmem((TILES, EDGE, WIDTH), F32),
        vmem((TILES * EDGE, WIDTH), F32),
        dma((12,)),
        dma((GROUP,)),
        dma((GROUP,)),
        dma,
        dma,
        dma((chunks,)),
        dma((chunks,)),
        dma((chunks,)),
        dma((chunks,)),
        dma((chunks + 1,)),
        dma((chunks + 1,)),
        dma((chunks + 1,)),
        dma((chunks + 1,)),
    ]
    return pl.pallas_call(
        kernel,
        out_shape=pltpu.VMEM((TILES * EDGE, WIDTH), BF16),
        in_specs=[pl.BlockSpec(memory_space=pl.ANY)] * len(operands),
        out_specs=pl.BlockSpec(memory_space=pltpu.VMEM),
        scratch_shapes=scratch,
        compiler_params=pltpu.CompilerParams(
            collective_id=0, has_side_effects=True, vmem_limit_bytes=40 * 2**20
        ),
        name="propagate",
    )(*operands)


def solution(mesh):
    both = ("dom", "blk")
    placed = (
        P(both, None),
        P(both, None),
        P(both),
        P(both, None, None, None, None),
        P(both, None, None),
        P(both, None, None),
        P(both, None, None),
        P(both, None, None, None),
        P(both, None),
        P(both, None),
    )
    return jax.shard_map(
        on_device, mesh=mesh, in_specs=placed, out_specs=P(both, None), check_vma=False
    )
```

```python
import jax
import jax.numpy as jnp
from jax import lax
from jax.experimental import pallas as pl
from jax.experimental.pallas import tpu as pltpu
from jax.sharding import PartitionSpec as P

ALPHA = 0.8
MESH = pl.DeviceIdType.MESH
F32 = jnp.float32
BF16 = jnp.bfloat16
I32 = jnp.int32
TILES = 16
EDGE = 128
WIDTH = 256
GRAIN = 16
PARTS = EDGE // GRAIN
GROUP = 8
SPAN = 4
UNITS = PARTS
RELAYS = tuple((u, h, TILES // 2) for u in range(UNITS) for h in (0, TILES // 2))
LAG = 4


def kernel(
    labels,
    tags,
    seeds,
    intra,
    cut,
    rows_hbm,
    cols_hbm,
    list_hbm,
    slot_hbm,
    crow_hbm,
    out,
    panel,
    prior,
    seedv,
    wi,
    wc,
    irows,
    icols,
    slist,
    cslot,
    crows,
    colmsg,
    listmsg,
    request_land,
    list_land,
    requests,
    partner_list,
    partner_parts,
    mirror_parts,
    x_stage_own,
    x_recv_own,
    x_stage,
    x_recv,
    z_stage_own,
    z_stage,
    z_recv,
    wmt,
    wm,
    lanes_m,
    degree,
    scale,
    base,
    total,
    local_sem,
    ask_send,
    ask_recv,
    list_send,
    list_recv,
    hop1_send,
    hop1_recv,
    hop2_send,
    hop2_recv,
    x_send,
    x_got,
    z_send,
    z_got,
):
    units = UNITS
    relays = len(RELAYS)
    own = units
    dom = lax.axis_index("dom")
    blk = lax.axis_index("blk")
    low, z = dom // GROUP, dom % GROUP
    high, j = blk // GROUP, blk % GROUP
    other_dom = (dom + GROUP) % (2 * GROUP)
    other_blk = (blk + GROUP) % (2 * GROUP)
    partner = (other_dom, blk)
    beyond = (other_dom, other_blk)

    def row_peer(d):
        return (dom, high * GROUP + (j + d) % GROUP)

    def z_peer(d):
        return (low * GROUP + (z + d) % GROUP, blk)

    def remote(src, dst, send, recv, device):
        return pltpu.make_async_remote_copy(
            src_ref=src,
            dst_ref=dst,
            send_sem=send,
            recv_sem=recv,
            device_id=device,
            device_id_type=MESH,
        )

    loads = [
        (cols_hbm, colmsg),
        (list_hbm, listmsg),
        (list_hbm, slist),
        (labels, panel),
        (cols_hbm, icols),
        (rows_hbm, irows),
        (intra, wi),
        (slot_hbm, cslot),
        (crow_hbm, crows),
        (seeds, seedv),
        (cut, wc),
        (tags, prior),
    ]
    loads = [
        pltpu.make_async_copy(src, dst, local_sem.at[i])
        for i, (src, dst) in enumerate(loads)
    ]

    barrier = pltpu.get_barrier_semaphore()

    def greet(d, carry):
        pl.semaphore_signal(barrier, inc=1, device_id=row_peer(d), device_id_type=MESH)
        pl.semaphore_signal(barrier, inc=1, device_id=z_peer(d), device_id_type=MESH)
        return carry

    pl.semaphore_signal(barrier, inc=1, device_id=partner, device_id_type=MESH)
    pl.semaphore_signal(barrier, inc=1, device_id=beyond, device_id_type=MESH)
    lax.fori_loop(1, GROUP, greet, 0)
    for load in loads:
        load.start()
    for load in loads[0:3]:
        load.wait()
    pl.semaphore_wait(barrier, 2 * GROUP)

    def ask(d):
        return remote(
            colmsg, request_land.at[d], ask_send.at[d], ask_recv.at[d], row_peer(d)
        )

    def start_ask(d, carry):
        ask(d).start()
        return carry

    lax.fori_loop(1, GROUP, start_ask, 0)
    tell = remote(listmsg, list_land, list_send, list_recv, partner)
    tell.start()

    def relay_refs(r):
        unit, first, count = RELAYS[r]
        at = pl.ds(first, count)
        return (
            labels.at[at, unit],
            partner_parts[unit].at[at],
            mirror_parts[unit].at[at],
        )

    hop1, hop2 = [], []
    for r in range(relays):
        here, there, far = relay_refs(r)
        hop1.append(remote(here, there, hop1_send.at[r], hop1_recv.at[r], partner))
        hop2.append(remote(there, far, hop2_send.at[r], hop2_recv.at[r], beyond))
    for r in range(relays):
        hop1[r].start()

    others = pl.ds(1, GROUP - 1)

    def spread_order(i):
        return 1 + (i + 3) % (GROUP - 1)

    def z_refs(index, at):
        if index == own:
            return z_stage_own.at[at], z_recv.at[0, at]
        return z_stage[index].at[at], z_recv.at[1, at, index]

    def x_refs(index, at):
        if index == own:
            return x_stage_own.at[at], x_recv_own.at[at]
        return x_stage[index].at[at], x_recv[index].at[at]

    def z_copy(index, at, d):
        src, dst = z_refs(index, at)
        return remote(src, dst, z_send.at[index], z_got.at[index], z_peer(d))

    def x_copy(index, at, d):
        src, dst = x_refs(index, at)
        return remote(src, dst, x_send.at[index], x_got.at[index], row_peer(d))

    def z_serve(source, wanted, index):
        stage = z_stage_own if index == own else z_stage[index]

        def one(i, carry):
            d = spread_order(i)
            stage[d] = source[wanted[0, low * GROUP + (z + d) % GROUP]]
            z_copy(index, d, d).start()
            return carry

        lax.fori_loop(0, GROUP - 1, one, 0)
        mine = source[wanted[0, dom]]
        if index == own:
            z_recv[0, 0] = mine
        else:
            z_recv[1, 0, index] = mine

    def x_serve(source, which, index):
        stage, recv = (
            (x_stage_own, x_recv_own)
            if index == own
            else (x_stage[index], x_recv[index])
        )

        def one(i, carry):
            d = spread_order(i)
            stage[d, 0] = source[requests[GROUP - d, 0, which]]
            stage[d, 1] = source[requests[GROUP - d, 1, which]]
            x_copy(index, d, d).start()
            return carry

        lax.fori_loop(0, GROUP - 1, one, 0)
        recv[0, 0] = source[icols[0, which]]
        recv[0, 1] = source[icols[1, which]]

    def z_wait(index):
        z_copy(index, others, 1).wait_recv()

    def x_wait(index):
        x_copy(index, others, 1).wait_recv()

    loads[3].wait()
    z_serve(panel, slist, own)

    def take_ask(d, carry):
        ask(d).wait_recv()
        return carry

    def serve_own_x():
        lax.fori_loop(1, GROUP, take_ask, 0)
        settle = pltpu.make_async_copy(request_land, requests, local_sem.at[0])
        settle.start()
        loads[4].wait()
        settle.wait()
        x_serve(panel, blk, own)

    def hear_list():
        tell.wait_recv()
        settle = pltpu.make_async_copy(list_land, partner_list, local_sem.at[1])
        settle.start()
        settle.wait()

    lane = lax.broadcasted_iota(I32, (GRAIN, 2 * EDGE), 1)

    def sender(d):
        return (j + GROUP - d) % GROUP

    def mirror_ids():
        loads[5].wait()
        loads[6].wait()
        slot = lane // GRAIN
        ids = jnp.zeros((GRAIN, 2 * EDGE), I32)
        for d in range(GROUP):
            for k in range(2):
                row = irows[k, (1 - high) * GROUP + sender(d)]
                ids = jnp.where(slot == 2 * d + k, row, ids)
        lanes_m[...] = ids

    def mirror_turn(first, count):
        def turn(d, carry):
            for k in range(2):
                flipped = wi[(1 - high) * GROUP + sender(d), k].T
                at = pl.ds(pl.multiple_of((2 * d + k) * GRAIN, GRAIN), GRAIN)
                for c in range(PARTS):
                    wmt[c, at, :] = flipped[c * GRAIN : (c + 1) * GRAIN, :]
            return carry

        lax.fori_loop(first, first + count, turn, 0)

    def mirror_back(first, count):
        def back(c, carry):
            wm[c, :, 0:EDGE] = wmt[c, 0:EDGE, :].T
            wm[c, :, EDGE : 2 * EDGE] = wmt[c, EDGE : 2 * EDGE, :].T
            return carry

        lax.fori_loop(first, first + count, back, 0)

    def sums(weights, row0, row1):
        tile = lax.broadcasted_iota(I32, (TILES, 2 * EDGE), 0)
        wide = lax.broadcasted_iota(I32, (TILES, 2 * EDGE), 1)
        chosen = jnp.where(tile == jnp.where(wide < EDGE, row0, row1), 1.0, 0.0)
        return lax.dot_general(
            weights,
            chosen.astype(BF16),
            (((1,), (1,)), ((), ())),
            preferred_element_type=F32,
        )

    def intra_degree(first, count):
        def one(s, value):
            weights = jnp.concatenate([wi[s, 0], wi[s, 1]], axis=1)
            return value + sums(weights, irows[0, s], irows[1, s])

        start = degree[...] if first else jnp.zeros((EDGE, TILES), F32)
        degree[...] = lax.fori_loop(first, first + count, one, start)

    def cut_degree():
        for load in loads[7:12]:
            load.wait()

        def one(h, value):
            weights = jnp.concatenate([wc[2 * h], wc[2 * h + 1]], axis=1)
            return value + sums(weights, crows[0, 2 * h], crows[0, 2 * h + 1])

        degree[...] = lax.fori_loop(0, TILES // 2, one, degree[...])

    def set_scale(first, count):
        mask = seedv[...].astype(F32).T
        factor = jnp.where(mask > 0.5, 0.0, ALPHA / degree[...])
        rest = jnp.where(mask > 0.5, 1.0, 1.0 - ALPHA)
        for t in range(first, first + count):
            scale[t] = jnp.broadcast_to(factor[:, t : t + 1], (EDGE, EDGE))
            share = jnp.broadcast_to(rest[:, t : t + 1], (EDGE, EDGE))
            share = jnp.concatenate([share, share], axis=1)
            base[t] = prior[t].astype(F32) * share

    def spread_part(tg, blocks):
        part = None
        for weights, ids, values in blocks:
            pieces = []
            width = weights.shape[1]
            cube = weights.reshape(PARTS, GRAIN, width)
            for u in range(SPAN):
                keep = jnp.where(ids == tg * SPAN + u, 1.0, 0.0).astype(BF16)
                pieces.append((cube * keep[None]).reshape(EDGE, width))
            lhs = jnp.concatenate(pieces, axis=0)
            term = jnp.dot(lhs, values, preferred_element_type=F32)
            part = term if part is None else part + term
        return part

    def row_span(tg):
        return pl.ds(pl.multiple_of(tg * SPAN * EDGE, EDGE), SPAN * EDGE)

    def own_x(first, count, lo, hi):
        def one(tg, carry):
            blocks = []
            for d in range(first, first + count):
                s = high * GROUP + sender(d)
                ids = jnp.where(lane < EDGE, irows[0, s], irows[1, s])
                weights = jnp.concatenate([wi[s, 0], wi[s, 1]], axis=1)
                values = x_recv_own[d].reshape(2 * EDGE, WIDTH)
                blocks.append((weights, ids, values))
            part = spread_part(tg, blocks)
            if first == 0:
                total[row_span(tg), :] = part
            else:
                total[row_span(tg), :] += part
            return carry

        lax.fori_loop(lo, hi, one, 0)

    def unit_block(u):
        return (wm[u], lanes_m[...], x_recv[u][...].reshape(2 * EDGE, WIDTH))

    def mirror_x(us, lo, hi):
        for u in us:
            x_wait(u)

        def one(tg, carry):
            blocks = [unit_block(u) for u in us]
            total[row_span(tg), :] += spread_part(tg, blocks)
            return carry

        lax.fori_loop(lo, hi, one, 0)

    def add_cut():
        def one(t, carry):
            k = (t + TILES - crows[0, 0]) % TILES
            q = cslot[0, k]
            group = jnp.where(q // GROUP == low, 0, 1)
            block = z_recv[group, (z + GROUP - q % GROUP) % GROUP]
            at = pl.ds(pl.multiple_of(t * EDGE, EDGE), EDGE)
            total[at, :] += jnp.dot(
                wc[k], block.reshape(EDGE, WIDTH), preferred_element_type=F32
            )
            return carry

        lax.fori_loop(0, TILES, one, 0, unroll=2)

    def finish(u):
        x_wait(u)

        def one(tg, carry):
            at = row_span(tg)
            spread = total[at, :] + spread_part(tg, [unit_block(u)])
            factor = scale[pl.ds(tg * SPAN, SPAN)].reshape(SPAN * EDGE, EDGE)
            factor = jnp.concatenate([factor, factor], axis=1)
            rest = base[pl.ds(tg * SPAN, SPAN)].reshape(SPAN * EDGE, WIDTH)
            out[at, :] = (factor * spread + rest).astype(BF16)
            return carry

        lax.fori_loop(0, TILES // SPAN, one, 0)

    work = {
        0: [(serve_own_x,)],
        2: [(mirror_ids,), (mirror_turn, 0, 4)],
        3: [(mirror_turn, 4, 4)],
        4: [(mirror_back, 0, 8)],
        6: [(intra_degree, 0, 8)],
        7: [(intra_degree, 8, 8)],
        8: [(cut_degree,)],
        9: [(set_scale, 0, 4)],
        10: [(set_scale, 4, 12)],
        11: [(x_wait, own), (own_x, 0, 4, 0, 1)],
        12: [(own_x, 0, 4, 1, 3)],
        13: [(own_x, 0, 4, 3, 4)],
        14: [(own_x, 4, 4, 0, 2)],
        15: [(own_x, 4, 4, 2, 3)],
        16: [(own_x, 4, 4, 3, 4)],
        17: [(mirror_x, (0, 1, 2), 0, 4)],
        18: [(mirror_x, (3, 4), 0, 4)],
    }
    last = [max(r for r in range(relays) if RELAYS[r][0] == u) for u in range(units)]
    for r in range(relays + LAG):
        if r < relays:
            hop1[r].wait_recv()
            hop2[r].start()
            if r == 0:
                hear_list()
            if r in last:
                z_serve(partner_parts[last.index(r)], partner_list, last.index(r))
        if r >= LAG:
            hop2[r - LAG].wait_recv()
            if r - LAG in last:
                u = last.index(r - LAG)
                x_serve(mirror_parts[u], other_blk, u)
        for piece, *given in work.get(r, []):
            piece(*given)
    z_wait(own)
    for u in range(units):
        z_wait(u)
    add_cut()
    mirror_x((5, 6), 0, 4)
    finish(7)

    def left(d, carry):
        ask(d).wait_send()
        return carry

    lax.fori_loop(1, GROUP, left, 0)
    tell.wait_send()
    for u in range(units + 1):
        z_copy(u, others, 1).wait_send()
        x_copy(u, others, 1).wait_send()
    for r in range(relays):
        hop1[r].wait_send()
        hop2[r].wait_send()


def on_device(
    labels,
    tags,
    seed_mask,
    intra_tiles,
    intra_rows,
    intra_cols,
    send_list,
    cut_tiles,
    cut_slot,
    cut_rows,
):
    units = UNITS
    relays = len(RELAYS)

    def flat(ids):
        return jnp.swapaxes(ids[0], 0, 1)

    operands = (
        labels.reshape(TILES, PARTS, GRAIN, WIDTH),
        tags.reshape(TILES, EDGE, WIDTH),
        seed_mask.reshape(TILES, EDGE),
        intra_tiles.reshape(TILES, 2, EDGE, EDGE),
        cut_tiles.reshape(TILES, EDGE, EDGE),
        flat(intra_rows),
        flat(intra_cols),
        flat(send_list),
        cut_slot,
        cut_rows,
    )
    operands = [pltpu.with_memory_space_constraint(x, pltpu.HBM) for x in operands]
    vmem = pltpu.VMEM
    smem = pltpu.SMEM
    dma = pltpu.SemaphoreType.DMA

    def per_unit(*shape):
        return [vmem((*shape, GRAIN, WIDTH), BF16) for _ in range(UNITS)]

    scratch = [
        vmem((TILES, PARTS, GRAIN, WIDTH), BF16),
        vmem((TILES, EDGE, WIDTH), BF16),
        vmem((TILES, EDGE), I32),
        vmem((TILES, 2, EDGE, EDGE), BF16),
        vmem((TILES, EDGE, EDGE), BF16),
        smem((2, TILES), I32),
        smem((2, TILES), I32),
        smem((1, TILES), I32),
        smem((1, TILES), I32),
        smem((1, TILES), I32),
        vmem((2, TILES), I32),
        vmem((1, TILES), I32),
        vmem((GROUP, 2, TILES), I32),
        vmem((1, TILES), I32),
        smem((GROUP, 2, TILES), I32),
        smem((1, TILES), I32),
        per_unit(TILES),
        per_unit(TILES),
        vmem((GROUP, 2, PARTS, GRAIN, WIDTH), BF16),
        vmem((GROUP, 2, PARTS, GRAIN, WIDTH), BF16),
        per_unit(GROUP, 2),
        per_unit(GROUP, 2),
        vmem((GROUP, PARTS, GRAIN, WIDTH), BF16),
        per_unit(GROUP),
        vmem((2, GROUP, PARTS, GRAIN, WIDTH), BF16),
        vmem((PARTS, 2 * EDGE, EDGE), BF16),
        vmem((PARTS, EDGE, 2 * EDGE), BF16),
        vmem((GRAIN, 2 * EDGE), I32),
        vmem((EDGE, TILES), F32),
        vmem((TILES, EDGE, EDGE), F32),
        vmem((TILES, EDGE, WIDTH), F32),
        vmem((TILES * EDGE, WIDTH), F32),
        dma((12,)),
        dma((GROUP,)),
        dma((GROUP,)),
        dma,
        dma,
        dma((relays,)),
        dma((relays,)),
        dma((relays,)),
        dma((relays,)),
        dma((units + 1,)),
        dma((units + 1,)),
        dma((units + 1,)),
        dma((units + 1,)),
    ]
    return pl.pallas_call(
        kernel,
        out_shape=pltpu.VMEM((TILES * EDGE, WIDTH), BF16),
        in_specs=[pl.BlockSpec(memory_space=pl.ANY)] * len(operands),
        out_specs=pl.BlockSpec(memory_space=pltpu.VMEM),
        scratch_shapes=scratch,
        compiler_params=pltpu.CompilerParams(
            collective_id=0, has_side_effects=True, vmem_limit_bytes=40 * 2**20
        ),
        name="propagate",
    )(*operands)


def solution(mesh):
    both = ("dom", "blk")
    placed = (
        P(both, None),
        P(both, None),
        P(both),
        P(both, None, None, None, None),
        P(both, None, None),
        P(both, None, None),
        P(both, None, None),
        P(both, None, None, None),
        P(both, None),
        P(both, None),
    )
    return jax.shard_map(
        on_device, mesh=mesh, in_specs=placed, out_specs=P(both, None), check_vma=False
    )
```

```python
import jax
import jax.numpy as jnp
from jax import lax
from jax.experimental import pallas as pl
from jax.experimental.pallas import tpu as pltpu
from jax.sharding import PartitionSpec as P

ALPHA = 0.8
MESH = pl.DeviceIdType.MESH
F32 = jnp.float32
BF16 = jnp.bfloat16
I32 = jnp.int32
TILES = 16
EDGE = 128
WIDTH = 256
GRAIN = 16
PARTS = EDGE // GRAIN
GROUP = 8
SPAN = 4
UNITS = PARTS
RELAYS = tuple((u, h, TILES // 2) for u in range(UNITS) for h in (0, TILES // 2))
LAG = 3


def kernel(
    labels,
    tags,
    seeds,
    intra,
    cut,
    rows_hbm,
    cols_hbm,
    list_hbm,
    slot_hbm,
    crow_hbm,
    out,
    panel,
    prior,
    seedv,
    wi,
    wc,
    irows,
    icols,
    slist,
    cslot,
    crows,
    colmsg,
    listmsg,
    request_land,
    list_land,
    requests,
    partner_list,
    partner_parts,
    mirror_parts,
    x_stage_own,
    x_recv_own,
    x_stage,
    x_recv,
    z_stage_own,
    z_stage,
    z_recv,
    wmt,
    wm,
    lanes_m,
    degree,
    scale,
    base,
    total,
    local_sem,
    ask_send,
    ask_recv,
    list_send,
    list_recv,
    hop1_send,
    hop1_recv,
    hop2_send,
    hop2_recv,
    x_send,
    x_got,
    z_send,
    z_got,
):
    units = UNITS
    relays = len(RELAYS)
    own = units
    dom = lax.axis_index("dom")
    blk = lax.axis_index("blk")
    low, z = dom // GROUP, dom % GROUP
    high, j = blk // GROUP, blk % GROUP
    other_dom = (dom + GROUP) % (2 * GROUP)
    other_blk = (blk + GROUP) % (2 * GROUP)
    partner = (other_dom, blk)
    beyond = (other_dom, other_blk)

    def row_peer(d):
        return (dom, high * GROUP + (j + d) % GROUP)

    def z_peer(d):
        return (low * GROUP + (z + d) % GROUP, blk)

    def remote(src, dst, send, recv, device):
        return pltpu.make_async_remote_copy(
            src_ref=src,
            dst_ref=dst,
            send_sem=send,
            recv_sem=recv,
            device_id=device,
            device_id_type=MESH,
        )

    loads = [
        (cols_hbm, colmsg),
        (list_hbm, listmsg),
        (list_hbm, slist),
        (labels, panel),
        (cols_hbm, icols),
        (rows_hbm, irows),
        (intra, wi),
        (slot_hbm, cslot),
        (crow_hbm, crows),
        (seeds, seedv),
        (cut, wc),
        (tags, prior),
    ]
    loads = [
        pltpu.make_async_copy(src, dst, local_sem.at[i])
        for i, (src, dst) in enumerate(loads)
    ]

    barrier = pltpu.get_barrier_semaphore()

    def greet(d, carry):
        pl.semaphore_signal(barrier, inc=1, device_id=row_peer(d), device_id_type=MESH)
        pl.semaphore_signal(barrier, inc=1, device_id=z_peer(d), device_id_type=MESH)
        return carry

    pl.semaphore_signal(barrier, inc=1, device_id=partner, device_id_type=MESH)
    pl.semaphore_signal(barrier, inc=1, device_id=beyond, device_id_type=MESH)
    lax.fori_loop(1, GROUP, greet, 0)
    for load in loads:
        load.start()
    for load in loads[0:3]:
        load.wait()
    pl.semaphore_wait(barrier, 2 * GROUP)

    def ask(d):
        return remote(
            colmsg, request_land.at[d], ask_send.at[d], ask_recv.at[d], row_peer(d)
        )

    def spread_order(i):
        return 1 + (i + 3) % (GROUP - 1)

    def start_ask(i, carry):
        ask(spread_order(i)).start()
        return carry

    lax.fori_loop(0, GROUP - 1, start_ask, 0)
    tell = remote(listmsg, list_land, list_send, list_recv, partner)
    tell.start()

    def relay_refs(r):
        unit, first, count = RELAYS[r]
        at = pl.ds(first, count)
        return (
            labels.at[at, unit],
            partner_parts[unit].at[at],
            mirror_parts[unit].at[at],
        )

    hop1, hop2 = [], []
    for r in range(relays):
        here, there, far = relay_refs(r)
        hop1.append(remote(here, there, hop1_send.at[r], hop1_recv.at[r], partner))
        hop2.append(remote(there, far, hop2_send.at[r], hop2_recv.at[r], beyond))
    for r in range(relays):
        hop1[r].start()

    others = pl.ds(1, GROUP - 1)

    def z_refs(index, at):
        if index == own:
            return z_stage_own.at[at], z_recv.at[0, at]
        return z_stage[index].at[at], z_recv.at[1, at, index]

    def x_refs(index, at):
        if index == own:
            return x_stage_own.at[at], x_recv_own.at[at]
        return x_stage[index].at[at], x_recv[index].at[at]

    def z_copy(index, at, d):
        src, dst = z_refs(index, at)
        return remote(src, dst, z_send.at[index], z_got.at[index], z_peer(d))

    def x_copy(index, at, d):
        src, dst = x_refs(index, at)
        return remote(src, dst, x_send.at[index], x_got.at[index], row_peer(d))

    def z_serve(source, wanted, index):
        stage = z_stage_own if index == own else z_stage[index]

        def one(i, carry):
            d = spread_order(i)
            stage[d] = source[wanted[0, low * GROUP + (z + d) % GROUP]]
            z_copy(index, d, d).start()
            return carry

        lax.fori_loop(0, GROUP - 1, one, 0)
        mine = source[wanted[0, dom]]
        if index == own:
            z_recv[0, 0] = mine
        else:
            z_recv[1, 0, index] = mine

    def x_serve(source, which, index):
        stage, recv = (
            (x_stage_own, x_recv_own)
            if index == own
            else (x_stage[index], x_recv[index])
        )

        def one(i, carry):
            d = spread_order(i)
            stage[d, 0] = source[requests[GROUP - d, 0, which]]
            stage[d, 1] = source[requests[GROUP - d, 1, which]]
            x_copy(index, d, d).start()
            return carry

        lax.fori_loop(0, GROUP - 1, one, 0)
        recv[0, 0] = source[icols[0, which]]
        recv[0, 1] = source[icols[1, which]]

    def z_wait(index):
        z_copy(index, others, 1).wait_recv()

    def x_wait(index):
        x_copy(index, others, 1).wait_recv()

    loads[3].wait()
    z_serve(panel, slist, own)

    def take_ask(d, carry):
        ask(d).wait_recv()
        return carry

    def serve_own_x():
        lax.fori_loop(1, GROUP, take_ask, 0)
        settle = pltpu.make_async_copy(request_land, requests, local_sem.at[0])
        settle.start()
        loads[4].wait()
        settle.wait()
        x_serve(panel, blk, own)

    def hear_list():
        tell.wait_recv()
        settle = pltpu.make_async_copy(list_land, partner_list, local_sem.at[1])
        settle.start()
        settle.wait()

    lane = lax.broadcasted_iota(I32, (GRAIN, 2 * EDGE), 1)

    def sender(d):
        return (j + GROUP - d) % GROUP

    def mirror_ids():
        loads[5].wait()
        loads[6].wait()
        slot = lane // GRAIN
        ids = jnp.zeros((GRAIN, 2 * EDGE), I32)
        for d in range(GROUP):
            for k in range(2):
                row = irows[k, (1 - high) * GROUP + sender(d)]
                ids = jnp.where(slot == 2 * d + k, row, ids)
        lanes_m[...] = ids

    def mirror_turn(first, count):
        def turn(d, carry):
            for k in range(2):
                flipped = wi[(1 - high) * GROUP + sender(d), k].T
                at = pl.ds(pl.multiple_of((2 * d + k) * GRAIN, GRAIN), GRAIN)
                for c in range(PARTS):
                    wmt[c, at, :] = flipped[c * GRAIN : (c + 1) * GRAIN, :]
            return carry

        lax.fori_loop(first, first + count, turn, 0)

    def mirror_back(first, count):
        def back(c, carry):
            wm[c, :, 0:EDGE] = wmt[c, 0:EDGE, :].T
            wm[c, :, EDGE : 2 * EDGE] = wmt[c, EDGE : 2 * EDGE, :].T
            return carry

        lax.fori_loop(first, first + count, back, 0)

    def sums(weights, row0, row1):
        tile = lax.broadcasted_iota(I32, (TILES, 2 * EDGE), 0)
        wide = lax.broadcasted_iota(I32, (TILES, 2 * EDGE), 1)
        chosen = jnp.where(tile == jnp.where(wide < EDGE, row0, row1), 1.0, 0.0)
        return lax.dot_general(
            weights,
            chosen.astype(BF16),
            (((1,), (1,)), ((), ())),
            preferred_element_type=F32,
        )

    def intra_degree(first, count):
        def one(s, value):
            weights = jnp.concatenate([wi[s, 0], wi[s, 1]], axis=1)
            return value + sums(weights, irows[0, s], irows[1, s])

        start = degree[...] if first else jnp.zeros((EDGE, TILES), F32)
        degree[...] = lax.fori_loop(first, first + count, one, start)

    def cut_degree():
        for load in loads[7:12]:
            load.wait()

        def one(h, value):
            weights = jnp.concatenate([wc[2 * h], wc[2 * h + 1]], axis=1)
            return value + sums(weights, crows[0, 2 * h], crows[0, 2 * h + 1])

        degree[...] = lax.fori_loop(0, TILES // 2, one, degree[...])

    def set_scale(first, count):
        mask = seedv[...].astype(F32).T
        factor = jnp.where(mask > 0.5, 0.0, ALPHA / degree[...])
        rest = jnp.where(mask > 0.5, 1.0, 1.0 - ALPHA)
        for t in range(first, first + count):
            scale[t] = jnp.broadcast_to(factor[:, t : t + 1], (EDGE, EDGE))
            share = jnp.broadcast_to(rest[:, t : t + 1], (EDGE, EDGE))
            share = jnp.concatenate([share, share], axis=1)
            base[t] = prior[t].astype(F32) * share

    def spread_part(tg, blocks):
        part = None
        for weights, ids, values in blocks:
            pieces = []
            width = weights.shape[1]
            cube = weights.reshape(PARTS, GRAIN, width)
            for u in range(SPAN):
                keep = jnp.where(ids == tg * SPAN + u, 1.0, 0.0).astype(BF16)
                pieces.append((cube * keep[None]).reshape(EDGE, width))
            lhs = jnp.concatenate(pieces, axis=0)
            term = jnp.dot(lhs, values, preferred_element_type=F32)
            part = term if part is None else part + term
        return part

    def row_span(tg):
        return pl.ds(pl.multiple_of(tg * SPAN * EDGE, EDGE), SPAN * EDGE)

    def own_x(first, count, lo, hi):
        def one(tg, carry):
            blocks = []
            for d in range(first, first + count):
                s = high * GROUP + sender(d)
                ids = jnp.where(lane < EDGE, irows[0, s], irows[1, s])
                weights = jnp.concatenate([wi[s, 0], wi[s, 1]], axis=1)
                values = x_recv_own[d].reshape(2 * EDGE, WIDTH)
                blocks.append((weights, ids, values))
            part = spread_part(tg, blocks)
            if first == 0:
                total[row_span(tg), :] = part
            else:
                total[row_span(tg), :] += part
            return carry

        lax.fori_loop(lo, hi, one, 0)

    def unit_block(u):
        return (wm[u], lanes_m[...], x_recv[u][...].reshape(2 * EDGE, WIDTH))

    def mirror_x(us, lo, hi):
        for u in us:
            x_wait(u)

        def one(tg, carry):
            blocks = [unit_block(u) for u in us]
            total[row_span(tg), :] += spread_part(tg, blocks)
            return carry

        lax.fori_loop(lo, hi, one, 0)

    def add_cut():
        def one(t, carry):
            k = (t + TILES - crows[0, 0]) % TILES
            q = cslot[0, k]
            group = jnp.where(q // GROUP == low, 0, 1)
            block = z_recv[group, (z + GROUP - q % GROUP) % GROUP]
            at = pl.ds(pl.multiple_of(t * EDGE, EDGE), EDGE)
            total[at, :] += jnp.dot(
                wc[k], block.reshape(EDGE, WIDTH), preferred_element_type=F32
            )
            return carry

        lax.fori_loop(0, TILES, one, 0, unroll=4)

    def finish(u):
        x_wait(u)

        def one(tg, carry):
            at = row_span(tg)
            spread = total[at, :] + spread_part(tg, [unit_block(u)])
            factor = scale[pl.ds(tg * SPAN, SPAN)].reshape(SPAN * EDGE, EDGE)
            factor = jnp.concatenate([factor, factor], axis=1)
            rest = base[pl.ds(tg * SPAN, SPAN)].reshape(SPAN * EDGE, WIDTH)
            out[at, :] = (factor * spread + rest).astype(BF16)
            return carry

        lax.fori_loop(0, TILES // SPAN, one, 0)

    work = {
        0: [(serve_own_x,)],
        2: [(mirror_ids,), (mirror_turn, 0, 2)],
        3: [(mirror_turn, 2, 2)],
        4: [(mirror_turn, 4, 4)],
        5: [(mirror_back, 0, 4)],
        6: [(mirror_back, 4, 4)],
        7: [(intra_degree, 0, 8)],
        8: [(intra_degree, 8, 8)],
        9: [(cut_degree,)],
        10: [(set_scale, 0, 8)],
        11: [(set_scale, 8, 8)],
        14: [(x_wait, own), (own_x, 0, 4, 0, 1), (own_x, 0, 4, 1, 2)],
        15: [(own_x, 0, 4, 2, 3), (own_x, 0, 4, 3, 4)],
        16: [(own_x, 4, 4, 0, 1), (own_x, 4, 4, 1, 2)],
        17: [(own_x, 4, 4, 2, 3), (own_x, 4, 4, 3, 4)],
        18: [(mirror_x, (0, 1, 2, 3), 0, 4)],
    }
    last = [max(r for r in range(relays) if RELAYS[r][0] == u) for u in range(units)]
    for r in range(relays + LAG):
        if r < relays:
            hop1[r].wait_recv()
            hop2[r].start()
            if r == 0:
                hear_list()
            if r in last:
                z_serve(partner_parts[last.index(r)], partner_list, last.index(r))
        if r >= LAG:
            hop2[r - LAG].wait_recv()
            if r - LAG in last:
                u = last.index(r - LAG)
                x_serve(mirror_parts[u], other_blk, u)
        for piece, *given in work.get(r, []):
            piece(*given)
    mirror_x((4, 5), 0, 4)
    z_wait(own)
    for u in range(units):
        z_wait(u)
    add_cut()
    mirror_x((6,), 0, 4)
    finish(7)

    def left(d, carry):
        ask(d).wait_send()
        return carry

    lax.fori_loop(1, GROUP, left, 0)
    tell.wait_send()
    for u in range(units + 1):
        z_copy(u, others, 1).wait_send()
        x_copy(u, others, 1).wait_send()
    for r in range(relays):
        hop1[r].wait_send()
        hop2[r].wait_send()


def on_device(
    labels,
    tags,
    seed_mask,
    intra_tiles,
    intra_rows,
    intra_cols,
    send_list,
    cut_tiles,
    cut_slot,
    cut_rows,
):
    units = UNITS
    relays = len(RELAYS)

    def flat(ids):
        return jnp.swapaxes(ids[0], 0, 1)

    operands = (
        labels.reshape(TILES, PARTS, GRAIN, WIDTH),
        tags.reshape(TILES, EDGE, WIDTH),
        seed_mask.reshape(TILES, EDGE),
        intra_tiles.reshape(TILES, 2, EDGE, EDGE),
        cut_tiles.reshape(TILES, EDGE, EDGE),
        flat(intra_rows),
        flat(intra_cols),
        flat(send_list),
        cut_slot,
        cut_rows,
    )
    operands = [pltpu.with_memory_space_constraint(x, pltpu.HBM) for x in operands]
    vmem = pltpu.VMEM
    smem = pltpu.SMEM
    dma = pltpu.SemaphoreType.DMA

    def per_unit(*shape):
        return [vmem((*shape, GRAIN, WIDTH), BF16) for _ in range(UNITS)]

    scratch = [
        vmem((TILES, PARTS, GRAIN, WIDTH), BF16),
        vmem((TILES, EDGE, WIDTH), BF16),
        vmem((TILES, EDGE), I32),
        vmem((TILES, 2, EDGE, EDGE), BF16),
        vmem((TILES, EDGE, EDGE), BF16),
        smem((2, TILES), I32),
        smem((2, TILES), I32),
        smem((1, TILES), I32),
        smem((1, TILES), I32),
        smem((1, TILES), I32),
        vmem((2, TILES), I32),
        vmem((1, TILES), I32),
        vmem((GROUP, 2, TILES), I32),
        vmem((1, TILES), I32),
        smem((GROUP, 2, TILES), I32),
        smem((1, TILES), I32),
        per_unit(TILES),
        per_unit(TILES),
        vmem((GROUP, 2, PARTS, GRAIN, WIDTH), BF16),
        vmem((GROUP, 2, PARTS, GRAIN, WIDTH), BF16),
        per_unit(GROUP, 2),
        per_unit(GROUP, 2),
        vmem((GROUP, PARTS, GRAIN, WIDTH), BF16),
        per_unit(GROUP),
        vmem((2, GROUP, PARTS, GRAIN, WIDTH), BF16),
        vmem((PARTS, 2 * EDGE, EDGE), BF16),
        vmem((PARTS, EDGE, 2 * EDGE), BF16),
        vmem((GRAIN, 2 * EDGE), I32),
        vmem((EDGE, TILES), F32),
        vmem((TILES, EDGE, EDGE), F32),
        vmem((TILES, EDGE, WIDTH), F32),
        vmem((TILES * EDGE, WIDTH), F32),
        dma((12,)),
        dma((GROUP,)),
        dma((GROUP,)),
        dma,
        dma,
        dma((relays,)),
        dma((relays,)),
        dma((relays,)),
        dma((relays,)),
        dma((units + 1,)),
        dma((units + 1,)),
        dma((units + 1,)),
        dma((units + 1,)),
    ]
    return pl.pallas_call(
        kernel,
        out_shape=pltpu.VMEM((TILES * EDGE, WIDTH), BF16),
        in_specs=[pl.BlockSpec(memory_space=pl.ANY)] * len(operands),
        out_specs=pl.BlockSpec(memory_space=pltpu.VMEM),
        scratch_shapes=scratch,
        compiler_params=pltpu.CompilerParams(
            collective_id=0, has_side_effects=True, vmem_limit_bytes=40 * 2**20
        ),
        name="propagate",
    )(*operands)


def solution(mesh):
    both = ("dom", "blk")
    placed = (
        P(both, None),
        P(both, None),
        P(both),
        P(both, None, None, None, None),
        P(both, None, None),
        P(both, None, None),
        P(both, None, None),
        P(both, None, None, None),
        P(both, None),
        P(both, None),
    )
    return jax.shard_map(
        on_device, mesh=mesh, in_specs=placed, out_specs=P(both, None), check_vma=False
    )
```

```python
import jax
import jax.numpy as jnp
from jax import lax
from jax.experimental import pallas as pl
from jax.experimental.pallas import tpu as pltpu
from jax.sharding import PartitionSpec as P

ALPHA = 0.8
MESH = pl.DeviceIdType.MESH
F32 = jnp.float32
BF16 = jnp.bfloat16
I32 = jnp.int32
TILES = 16
EDGE = 128
WIDTH = 256
GRAIN = 16
PARTS = EDGE // GRAIN
GROUP = 8
SPAN = 4
UNITS = PARTS
RELAYS = tuple((u, h, TILES // 2) for u in range(UNITS) for h in (0, TILES // 2))
LAG = 3


def kernel(
    labels,
    tags,
    seeds,
    intra,
    cut,
    rows_hbm,
    cols_hbm,
    list_hbm,
    slot_hbm,
    crow_hbm,
    out,
    panel,
    prior,
    seedv,
    wi,
    wc,
    irows,
    icols,
    slist,
    cslot,
    crows,
    colmsg,
    listmsg,
    request_land,
    list_land,
    requests,
    partner_list,
    partner_parts,
    mirror_parts,
    x_stage_own,
    x_recv_own,
    x_stage,
    x_recv,
    z_stage_own,
    z_stage,
    z_recv,
    wmt,
    wm,
    lanes_m,
    degree,
    scale,
    base,
    total,
    local_sem,
    ask_send,
    ask_recv,
    list_send,
    list_recv,
    hop1_send,
    hop1_recv,
    hop2_send,
    hop2_recv,
    x_send,
    x_got,
    z_send,
    z_got,
):
    units = UNITS
    relays = len(RELAYS)
    own = units
    dom = lax.axis_index("dom")
    blk = lax.axis_index("blk")
    low, z = dom // GROUP, dom % GROUP
    high, j = blk // GROUP, blk % GROUP
    other_dom = (dom + GROUP) % (2 * GROUP)
    other_blk = (blk + GROUP) % (2 * GROUP)
    partner = (other_dom, blk)
    beyond = (other_dom, other_blk)

    def row_peer(d):
        return (dom, high * GROUP + (j + d) % GROUP)

    def z_peer(d):
        return (low * GROUP + (z + d) % GROUP, blk)

    def remote(src, dst, send, recv, device):
        return pltpu.make_async_remote_copy(
            src_ref=src,
            dst_ref=dst,
            send_sem=send,
            recv_sem=recv,
            device_id=device,
            device_id_type=MESH,
        )

    loads = [
        (cols_hbm, colmsg),
        (list_hbm, listmsg),
        (list_hbm, slist),
        (labels, panel),
        (cols_hbm, icols),
        (rows_hbm, irows),
        (intra, wi),
        (slot_hbm, cslot),
        (crow_hbm, crows),
        (seeds, seedv),
        (cut, wc),
        (tags, prior),
    ]
    loads = [
        pltpu.make_async_copy(src, dst, local_sem.at[i])
        for i, (src, dst) in enumerate(loads)
    ]

    barrier = pltpu.get_barrier_semaphore()

    def greet(d, carry):
        pl.semaphore_signal(barrier, inc=1, device_id=row_peer(d), device_id_type=MESH)
        pl.semaphore_signal(barrier, inc=1, device_id=z_peer(d), device_id_type=MESH)
        return carry

    pl.semaphore_signal(barrier, inc=1, device_id=partner, device_id_type=MESH)
    pl.semaphore_signal(barrier, inc=1, device_id=beyond, device_id_type=MESH)
    lax.fori_loop(1, GROUP, greet, 0)
    for load in loads:
        load.start()
    for load in loads[0:3]:
        load.wait()
    pl.semaphore_wait(barrier, 2 * GROUP)

    def ask(d):
        return remote(
            colmsg, request_land.at[d], ask_send, ask_recv, row_peer(d)
        )

    def spread_order(i):
        return 1 + (i + 3) % (GROUP - 1)

    def start_ask(i, carry):
        ask(spread_order(i)).start()
        return carry

    lax.fori_loop(0, GROUP - 1, start_ask, 0)
    tell = remote(listmsg, list_land, list_send, list_recv, partner)
    tell.start()

    def relay_refs(r):
        unit, first, count = RELAYS[r]
        at = pl.ds(first, count)
        return (
            labels.at[at, unit],
            partner_parts[unit].at[at],
            mirror_parts[unit].at[at],
        )

    hop1, hop2 = [], []
    for r in range(relays):
        here, there, far = relay_refs(r)
        hop1.append(remote(here, there, hop1_send, hop1_recv.at[r], partner))
        hop2.append(remote(there, far, hop2_send, hop2_recv.at[r], beyond))
    for r in range(relays):
        hop1[r].start()

    others = pl.ds(1, GROUP - 1)

    def z_refs(index, at):
        if index == own:
            return z_stage_own.at[at], z_recv.at[0, at]
        return z_stage[index].at[at], z_recv.at[1, at, index]

    def x_refs(index, at):
        if index == own:
            return x_stage_own.at[at], x_recv_own.at[at]
        return x_stage[index].at[at], x_recv[index].at[at]

    def z_copy(index, at, d):
        src, dst = z_refs(index, at)
        return remote(src, dst, z_send.at[index], z_got.at[index], z_peer(d))

    def x_copy(index, at, d):
        src, dst = x_refs(index, at)
        return remote(src, dst, x_send.at[index], x_got.at[index], row_peer(d))

    def z_serve(source, wanted, index):
        stage = z_stage_own if index == own else z_stage[index]

        def one(i, carry):
            d = spread_order(i)
            stage[d] = source[wanted[0, low * GROUP + (z + d) % GROUP]]
            z_copy(index, d, d).start()
            return carry

        lax.fori_loop(0, GROUP - 1, one, 0)
        mine = source[wanted[0, dom]]
        if index == own:
            z_recv[0, 0] = mine
        else:
            z_recv[1, 0, index] = mine

    def x_serve(source, which, index):
        stage, recv = (
            (x_stage_own, x_recv_own)
            if index == own
            else (x_stage[index], x_recv[index])
        )

        def one(i, carry):
            d = spread_order(i)
            stage[d, 0] = source[requests[GROUP - d, 0, which]]
            stage[d, 1] = source[requests[GROUP - d, 1, which]]
            x_copy(index, d, d).start()
            return carry

        lax.fori_loop(0, GROUP - 1, one, 0)
        recv[0, 0] = source[icols[0, which]]
        recv[0, 1] = source[icols[1, which]]

    def z_wait(index):
        z_copy(index, others, 1).wait_recv()

    def x_wait(index):
        x_copy(index, others, 1).wait_recv()

    loads[3].wait()
    z_serve(panel, slist, own)

    def all_asks():
        landed = request_land.at[others]
        return remote(landed, landed, ask_send, ask_recv, row_peer(1))

    def serve_own_x():
        all_asks().wait_recv()
        settle = pltpu.make_async_copy(request_land, requests, local_sem.at[0])
        settle.start()
        loads[4].wait()
        settle.wait()
        x_serve(panel, blk, own)

    def hear_list():
        tell.wait_recv()
        settle = pltpu.make_async_copy(list_land, partner_list, local_sem.at[1])
        settle.start()
        settle.wait()

    lane = lax.broadcasted_iota(I32, (GRAIN, 2 * EDGE), 1)

    def sender(d):
        return (j + GROUP - d) % GROUP

    def mirror_ids():
        loads[5].wait()
        loads[6].wait()
        slot = lane // GRAIN
        ids = jnp.zeros((GRAIN, 2 * EDGE), I32)
        for d in range(GROUP):
            for k in range(2):
                row = irows[k, (1 - high) * GROUP + sender(d)]
                ids = jnp.where(slot == 2 * d + k, row, ids)
        lanes_m[...] = ids

    def mirror_turn(first, count):
        def turn(d, carry):
            for k in range(2):
                flipped = wi[(1 - high) * GROUP + sender(d), k].T
                at = pl.ds(pl.multiple_of((2 * d + k) * GRAIN, GRAIN), GRAIN)
                for c in range(PARTS):
                    wmt[c, at, :] = flipped[c * GRAIN : (c + 1) * GRAIN, :]
            return carry

        lax.fori_loop(first, first + count, turn, 0)

    def mirror_back(first, count):
        def back(c, carry):
            wm[c, :, 0:EDGE] = wmt[c, 0:EDGE, :].T
            wm[c, :, EDGE : 2 * EDGE] = wmt[c, EDGE : 2 * EDGE, :].T
            return carry

        lax.fori_loop(first, first + count, back, 0)

    def sums(weights, row0, row1):
        tile = lax.broadcasted_iota(I32, (TILES, 2 * EDGE), 0)
        wide = lax.broadcasted_iota(I32, (TILES, 2 * EDGE), 1)
        chosen = jnp.where(tile == jnp.where(wide < EDGE, row0, row1), 1.0, 0.0)
        return lax.dot_general(
            weights,
            chosen.astype(BF16),
            (((1,), (1,)), ((), ())),
            preferred_element_type=F32,
        )

    def intra_degree(first, count):
        def one(s, value):
            weights = jnp.concatenate([wi[s, 0], wi[s, 1]], axis=1)
            return value + sums(weights, irows[0, s], irows[1, s])

        start = degree[...] if first else jnp.zeros((EDGE, TILES), F32)
        degree[...] = lax.fori_loop(first, first + count, one, start)

    def cut_degree():
        for load in loads[7:12]:
            load.wait()

        def one(h, value):
            weights = jnp.concatenate([wc[2 * h], wc[2 * h + 1]], axis=1)
            return value + sums(weights, crows[0, 2 * h], crows[0, 2 * h + 1])

        degree[...] = lax.fori_loop(0, TILES // 2, one, degree[...])

    def set_scale(first, count):
        mask = seedv[...].astype(F32).T
        factor = jnp.where(mask > 0.5, 0.0, ALPHA / degree[...])
        rest = jnp.where(mask > 0.5, 1.0, 1.0 - ALPHA)
        for t in range(first, first + count):
            scale[t] = jnp.broadcast_to(factor[:, t : t + 1], (EDGE, EDGE))
            share = jnp.broadcast_to(rest[:, t : t + 1], (EDGE, EDGE))
            share = jnp.concatenate([share, share], axis=1)
            base[t] = prior[t].astype(F32) * share

    def spread_part(tg, blocks):
        part = None
        for weights, ids, values in blocks:
            pieces = []
            width = weights.shape[1]
            cube = weights.reshape(PARTS, GRAIN, width)
            for u in range(SPAN):
                keep = jnp.where(ids == tg * SPAN + u, 1.0, 0.0).astype(BF16)
                pieces.append((cube * keep[None]).reshape(EDGE, width))
            lhs = jnp.concatenate(pieces, axis=0)
            term = jnp.dot(lhs, values, preferred_element_type=F32)
            part = term if part is None else part + term
        return part

    def row_span(tg):
        return pl.ds(pl.multiple_of(tg * SPAN * EDGE, EDGE), SPAN * EDGE)

    def own_x(first, count, lo, hi):
        def one(tg, carry):
            blocks = []
            for d in range(first, first + count):
                s = high * GROUP + sender(d)
                ids = jnp.where(lane < EDGE, irows[0, s], irows[1, s])
                weights = jnp.concatenate([wi[s, 0], wi[s, 1]], axis=1)
                values = x_recv_own[d].reshape(2 * EDGE, WIDTH)
                blocks.append((weights, ids, values))
            part = spread_part(tg, blocks)
            if first == 0:
                total[row_span(tg), :] = part
            else:
                total[row_span(tg), :] += part
            return carry

        lax.fori_loop(lo, hi, one, 0)

    def unit_block(u):
        return (wm[u], lanes_m[...], x_recv[u][...].reshape(2 * EDGE, WIDTH))

    def mirror_x(us, lo, hi):
        for u in us:
            x_wait(u)

        def one(tg, carry):
            blocks = [unit_block(u) for u in us]
            total[row_span(tg), :] += spread_part(tg, blocks)
            return carry

        lax.fori_loop(lo, hi, one, 0)

    def add_cut():
        def one(t, carry):
            k = (t + TILES - crows[0, 0]) % TILES
            q = cslot[0, k]
            group = jnp.where(q // GROUP == low, 0, 1)
            block = z_recv[group, (z + GROUP - q % GROUP) % GROUP]
            at = pl.ds(pl.multiple_of(t * EDGE, EDGE), EDGE)
            total[at, :] += jnp.dot(
                wc[k], block.reshape(EDGE, WIDTH), preferred_element_type=F32
            )
            return carry

        lax.fori_loop(0, TILES, one, 0, unroll=4)

    def finish(u):
        x_wait(u)

        def one(tg, carry):
            at = row_span(tg)
            spread = total[at, :] + spread_part(tg, [unit_block(u)])
            factor = scale[pl.ds(tg * SPAN, SPAN)].reshape(SPAN * EDGE, EDGE)
            factor = jnp.concatenate([factor, factor], axis=1)
            rest = base[pl.ds(tg * SPAN, SPAN)].reshape(SPAN * EDGE, WIDTH)
            out[at, :] = (factor * spread + rest).astype(BF16)
            return carry

        lax.fori_loop(0, TILES // SPAN, one, 0)

    work = {
        0: [(serve_own_x,)],
        2: [(mirror_ids,), (mirror_turn, 0, 2)],
        3: [(mirror_turn, 2, 2)],
        4: [(mirror_turn, 4, 4)],
        5: [(mirror_back, 0, 4)],
        6: [(mirror_back, 4, 4)],
        7: [(intra_degree, 0, 8)],
        8: [(intra_degree, 8, 8)],
        9: [(cut_degree,)],
        10: [(set_scale, 0, 8)],
        11: [(set_scale, 8, 8)],
        14: [(x_wait, own), (own_x, 0, 4, 0, 1), (own_x, 0, 4, 1, 2)],
        15: [(own_x, 0, 4, 2, 3), (own_x, 0, 4, 3, 4)],
        16: [(own_x, 4, 4, 0, 1), (own_x, 4, 4, 1, 2)],
        17: [(own_x, 4, 4, 2, 3), (own_x, 4, 4, 3, 4)],
        18: [(mirror_x, (0, 1, 2, 3), 0, 4)],
    }
    last = [max(r for r in range(relays) if RELAYS[r][0] == u) for u in range(units)]
    for r in range(relays + LAG):
        if r < relays:
            hop1[r].wait_recv()
            hop2[r].start()
            if r == 0:
                hear_list()
            if r in last:
                z_serve(partner_parts[last.index(r)], partner_list, last.index(r))
        if r >= LAG:
            hop2[r - LAG].wait_recv()
            if r - LAG in last:
                u = last.index(r - LAG)
                x_serve(mirror_parts[u], other_blk, u)
        for piece, *given in work.get(r, []):
            piece(*given)
    mirror_x((4, 5), 0, 4)
    z_wait(own)
    for u in range(units):
        z_wait(u)
    add_cut()
    mirror_x((6,), 0, 4)
    finish(7)

    all_asks().wait_send()
    tell.wait_send()
    for u in range(units + 1):
        z_copy(u, others, 1).wait_send()
        x_copy(u, others, 1).wait_send()
    remote(labels, panel, hop1_send, hop1_recv.at[0], partner).wait_send()
    remote(panel, panel, hop2_send, hop2_recv.at[0], beyond).wait_send()


def on_device(
    labels,
    tags,
    seed_mask,
    intra_tiles,
    intra_rows,
    intra_cols,
    send_list,
    cut_tiles,
    cut_slot,
    cut_rows,
):
    units = UNITS
    relays = len(RELAYS)

    def flat(ids):
        return jnp.swapaxes(ids[0], 0, 1)

    operands = (
        labels.reshape(TILES, PARTS, GRAIN, WIDTH),
        tags.reshape(TILES, EDGE, WIDTH),
        seed_mask.reshape(TILES, EDGE),
        intra_tiles.reshape(TILES, 2, EDGE, EDGE),
        cut_tiles.reshape(TILES, EDGE, EDGE),
        flat(intra_rows),
        flat(intra_cols),
        flat(send_list),
        cut_slot,
        cut_rows,
    )
    operands = [pltpu.with_memory_space_constraint(x, pltpu.HBM) for x in operands]
    vmem = pltpu.VMEM
    smem = pltpu.SMEM
    dma = pltpu.SemaphoreType.DMA

    def per_unit(*shape):
        return [vmem((*shape, GRAIN, WIDTH), BF16) for _ in range(UNITS)]

    scratch = [
        vmem((TILES, PARTS, GRAIN, WIDTH), BF16),
        vmem((TILES, EDGE, WIDTH), BF16),
        vmem((TILES, EDGE), I32),
        vmem((TILES, 2, EDGE, EDGE), BF16),
        vmem((TILES, EDGE, EDGE), BF16),
        smem((2, TILES), I32),
        smem((2, TILES), I32),
        smem((1, TILES), I32),
        smem((1, TILES), I32),
        smem((1, TILES), I32),
        vmem((2, TILES), I32),
        vmem((1, TILES), I32),
        vmem((GROUP, 2, TILES), I32),
        vmem((1, TILES), I32),
        smem((GROUP, 2, TILES), I32),
        smem((1, TILES), I32),
        per_unit(TILES),
        per_unit(TILES),
        vmem((GROUP, 2, PARTS, GRAIN, WIDTH), BF16),
        vmem((GROUP, 2, PARTS, GRAIN, WIDTH), BF16),
        per_unit(GROUP, 2),
        per_unit(GROUP, 2),
        vmem((GROUP, PARTS, GRAIN, WIDTH), BF16),
        per_unit(GROUP),
        vmem((2, GROUP, PARTS, GRAIN, WIDTH), BF16),
        vmem((PARTS, 2 * EDGE, EDGE), BF16),
        vmem((PARTS, EDGE, 2 * EDGE), BF16),
        vmem((GRAIN, 2 * EDGE), I32),
        vmem((EDGE, TILES), F32),
        vmem((TILES, EDGE, EDGE), F32),
        vmem((TILES, EDGE, WIDTH), F32),
        vmem((TILES * EDGE, WIDTH), F32),
        dma((12,)),
        dma,
        dma,
        dma,
        dma,
        dma,
        dma((relays,)),
        dma,
        dma((relays,)),
        dma((units + 1,)),
        dma((units + 1,)),
        dma((units + 1,)),
        dma((units + 1,)),
    ]
    return pl.pallas_call(
        kernel,
        out_shape=pltpu.VMEM((TILES * EDGE, WIDTH), BF16),
        in_specs=[pl.BlockSpec(memory_space=pl.ANY)] * len(operands),
        out_specs=pl.BlockSpec(memory_space=pltpu.VMEM),
        scratch_shapes=scratch,
        compiler_params=pltpu.CompilerParams(
            collective_id=0, has_side_effects=True, vmem_limit_bytes=40 * 2**20
        ),
        name="propagate",
    )(*operands)


def solution(mesh):
    both = ("dom", "blk")
    placed = (
        P(both, None),
        P(both, None),
        P(both),
        P(both, None, None, None, None),
        P(both, None, None),
        P(both, None, None),
        P(both, None, None),
        P(both, None, None, None),
        P(both, None),
        P(both, None),
    )
    return jax.shard_map(
        on_device, mesh=mesh, in_specs=placed, out_specs=P(both, None), check_vma=False
    )
```

```python
import jax
import jax.numpy as jnp
from jax import lax
from jax.experimental import pallas as pl
from jax.experimental.pallas import tpu as pltpu
from jax.sharding import PartitionSpec as P

ALPHA = 0.8
MESH = pl.DeviceIdType.MESH
F32 = jnp.float32
BF16 = jnp.bfloat16
I32 = jnp.int32
TILES = 16
EDGE = 128
WIDTH = 256
GRAIN = 16
PARTS = EDGE // GRAIN
GROUP = 8
SPAN = 4
UNITS = PARTS
RELAYS = tuple((u, h, TILES // 2) for u in range(UNITS) for h in (0, TILES // 2))
LAG = 3


def kernel(
    labels,
    tags,
    seeds,
    intra,
    cut,
    rows_hbm,
    cols_hbm,
    list_hbm,
    slot_hbm,
    crow_hbm,
    out,
    panel,
    prior,
    seedv,
    wi,
    wc,
    irows,
    icols,
    slist,
    cslot,
    crows,
    colmsg,
    listmsg,
    request_land,
    list_land,
    requests,
    partner_list,
    partner_parts,
    mirror_parts,
    x_stage_own,
    x_recv_own,
    x_stage,
    x_recv,
    z_stage_own,
    z_stage,
    z_recv,
    wmt,
    wm,
    lanes_m,
    degree,
    scale,
    base,
    total,
    local_sem,
    ask_send,
    ask_recv,
    list_send,
    list_recv,
    hop1_send,
    hop1_recv,
    hop2_send,
    hop2_recv,
    x_send,
    x_got,
    z_send,
    z_got,
):
    units = UNITS
    relays = len(RELAYS)
    own = units
    dom = lax.axis_index("dom")
    blk = lax.axis_index("blk")
    low, z = dom // GROUP, dom % GROUP
    high, j = blk // GROUP, blk % GROUP
    other_dom = (dom + GROUP) % (2 * GROUP)
    other_blk = (blk + GROUP) % (2 * GROUP)
    partner = (other_dom, blk)
    beyond = (other_dom, other_blk)

    def row_peer(d):
        return (dom, high * GROUP + (j + d) % GROUP)

    def z_peer(d):
        return (low * GROUP + (z + d) % GROUP, blk)

    def remote(src, dst, send, recv, device):
        return pltpu.make_async_remote_copy(
            src_ref=src,
            dst_ref=dst,
            send_sem=send,
            recv_sem=recv,
            device_id=device,
            device_id_type=MESH,
        )

    loads = [
        (cols_hbm, colmsg),
        (list_hbm, listmsg),
        (list_hbm, slist),
        (labels, panel),
        (cols_hbm, icols),
        (rows_hbm, irows),
        (intra, wi),
        (slot_hbm, cslot),
        (crow_hbm, crows),
        (seeds, seedv),
        (cut, wc),
        (tags, prior),
    ]
    loads = [
        pltpu.make_async_copy(src, dst, local_sem.at[i])
        for i, (src, dst) in enumerate(loads)
    ]

    barrier = pltpu.get_barrier_semaphore()

    def greet(d, carry):
        pl.semaphore_signal(barrier, inc=1, device_id=row_peer(d), device_id_type=MESH)
        pl.semaphore_signal(barrier, inc=1, device_id=z_peer(d), device_id_type=MESH)
        return carry

    pl.semaphore_signal(barrier, inc=1, device_id=partner, device_id_type=MESH)
    pl.semaphore_signal(barrier, inc=1, device_id=beyond, device_id_type=MESH)
    lax.fori_loop(1, GROUP, greet, 0)
    for load in loads:
        load.start()
    for load in loads[0:3]:
        load.wait()
    pl.semaphore_wait(barrier, 2 * GROUP)

    def ask(d):
        return remote(
            colmsg, request_land.at[d], ask_send, ask_recv, row_peer(d)
        )

    def spread_order(i):
        return 1 + (i + 3) % (GROUP - 1)

    def start_ask(i, carry):
        ask(spread_order(i)).start()
        return carry

    lax.fori_loop(0, GROUP - 1, start_ask, 0)
    tell = remote(listmsg, list_land, list_send, list_recv, partner)
    tell.start()

    def relay_refs(r):
        unit, first, count = RELAYS[r]
        at = pl.ds(first, count)
        return (
            labels.at[at, unit],
            partner_parts[unit].at[at],
            mirror_parts[unit].at[at],
        )

    hop1, hop2 = [], []
    for r in range(relays):
        here, there, far = relay_refs(r)
        hop1.append(remote(here, there, hop1_send, hop1_recv.at[r], partner))
        hop2.append(remote(there, far, hop2_send, hop2_recv.at[r], beyond))
    for r in range(relays):
        hop1[r].start()

    others = pl.ds(1, GROUP - 1)

    def z_refs(index, at):
        if index == own:
            return z_stage_own.at[at], z_recv.at[0, at]
        return z_stage[index].at[at], z_recv.at[1, at, index]

    def x_refs(index, at):
        if index == own:
            return x_stage_own.at[at], x_recv_own.at[at]
        return x_stage[index].at[at], x_recv[index].at[at]

    def z_copy(index, at, d):
        src, dst = z_refs(index, at)
        return remote(src, dst, z_send, z_got.at[index], z_peer(d))

    def x_copy(index, at, d):
        src, dst = x_refs(index, at)
        return remote(src, dst, x_send, x_got.at[index], row_peer(d))

    def z_serve(source, wanted, index):
        stage = z_stage_own if index == own else z_stage[index]

        def one(i, carry):
            d = spread_order(i)
            stage[d] = source[wanted[0, low * GROUP + (z + d) % GROUP]]
            z_copy(index, d, d).start()
            return carry

        lax.fori_loop(0, GROUP - 1, one, 0)
        mine = source[wanted[0, dom]]
        if index == own:
            z_recv[0, 0] = mine
        else:
            z_recv[1, 0, index] = mine

    def x_serve(source, which, index):
        stage, recv = (
            (x_stage_own, x_recv_own)
            if index == own
            else (x_stage[index], x_recv[index])
        )

        def one(i, carry):
            d = spread_order(i)
            stage[d, 0] = source[requests[GROUP - d, 0, which]]
            stage[d, 1] = source[requests[GROUP - d, 1, which]]
            x_copy(index, d, d).start()
            return carry

        lax.fori_loop(0, GROUP - 1, one, 0)
        recv[0, 0] = source[icols[0, which]]
        recv[0, 1] = source[icols[1, which]]

    def z_wait(index):
        z_copy(index, others, 1).wait_recv()

    def x_wait(index):
        x_copy(index, others, 1).wait_recv()

    loads[3].wait()
    z_serve(panel, slist, own)

    def all_asks():
        landed = request_land.at[others]
        return remote(landed, landed, ask_send, ask_recv, row_peer(1))

    def serve_own_x():
        all_asks().wait_recv()
        settle = pltpu.make_async_copy(request_land, requests, local_sem.at[0])
        settle.start()
        loads[4].wait()
        settle.wait()
        x_serve(panel, blk, own)

    def hear_list():
        tell.wait_recv()
        settle = pltpu.make_async_copy(list_land, partner_list, local_sem.at[1])
        settle.start()
        settle.wait()

    lane = lax.broadcasted_iota(I32, (GRAIN, 2 * EDGE), 1)

    def sender(d):
        return (j + GROUP - d) % GROUP

    def mirror_ids():
        loads[5].wait()
        loads[6].wait()
        slot = lane // GRAIN
        ids = jnp.zeros((GRAIN, 2 * EDGE), I32)
        for d in range(GROUP):
            for k in range(2):
                row = irows[k, (1 - high) * GROUP + sender(d)]
                ids = jnp.where(slot == 2 * d + k, row, ids)
        lanes_m[...] = ids

    def mirror_turn(first, count):
        def turn(d, carry):
            for k in range(2):
                flipped = wi[(1 - high) * GROUP + sender(d), k].T
                at = pl.ds(pl.multiple_of((2 * d + k) * GRAIN, GRAIN), GRAIN)
                for c in range(PARTS):
                    wmt[c, at, :] = flipped[c * GRAIN : (c + 1) * GRAIN, :]
            return carry

        lax.fori_loop(first, first + count, turn, 0)

    def mirror_back(first, count):
        def back(c, carry):
            wm[c, :, 0:EDGE] = wmt[c, 0:EDGE, :].T
            wm[c, :, EDGE : 2 * EDGE] = wmt[c, EDGE : 2 * EDGE, :].T
            return carry

        lax.fori_loop(first, first + count, back, 0)

    def sums(weights, row0, row1):
        tile = lax.broadcasted_iota(I32, (TILES, 2 * EDGE), 0)
        wide = lax.broadcasted_iota(I32, (TILES, 2 * EDGE), 1)
        chosen = jnp.where(tile == jnp.where(wide < EDGE, row0, row1), 1.0, 0.0)
        return lax.dot_general(
            weights,
            chosen.astype(BF16),
            (((1,), (1,)), ((), ())),
            preferred_element_type=F32,
        )

    def intra_degree(first, count):
        def one(s, value):
            weights = jnp.concatenate([wi[s, 0], wi[s, 1]], axis=1)
            return value + sums(weights, irows[0, s], irows[1, s])

        start = degree[...] if first else jnp.zeros((EDGE, TILES), F32)
        degree[...] = lax.fori_loop(first, first + count, one, start)

    def cut_degree():
        for load in loads[7:12]:
            load.wait()

        def one(h, value):
            weights = jnp.concatenate([wc[2 * h], wc[2 * h + 1]], axis=1)
            return value + sums(weights, crows[0, 2 * h], crows[0, 2 * h + 1])

        degree[...] = lax.fori_loop(0, TILES // 2, one, degree[...])

    def set_scale(first, count):
        mask = seedv[...].astype(F32).T
        factor = jnp.where(mask > 0.5, 0.0, ALPHA / degree[...])
        rest = jnp.where(mask > 0.5, 1.0, 1.0 - ALPHA)
        for t in range(first, first + count):
            scale[t] = jnp.broadcast_to(factor[:, t : t + 1], (EDGE, EDGE))
            share = jnp.broadcast_to(rest[:, t : t + 1], (EDGE, EDGE))
            share = jnp.concatenate([share, share], axis=1)
            base[t] = prior[t].astype(F32) * share

    def spread_part(tg, blocks):
        part = None
        for weights, ids, values in blocks:
            pieces = []
            width = weights.shape[1]
            cube = weights.reshape(PARTS, GRAIN, width)
            for u in range(SPAN):
                keep = jnp.where(ids == tg * SPAN + u, 1.0, 0.0).astype(BF16)
                pieces.append((cube * keep[None]).reshape(EDGE, width))
            lhs = jnp.concatenate(pieces, axis=0)
            term = jnp.dot(lhs, values, preferred_element_type=F32)
            part = term if part is None else part + term
        return part

    def row_span(tg):
        return pl.ds(pl.multiple_of(tg * SPAN * EDGE, EDGE), SPAN * EDGE)

    def own_x(first, count, lo, hi):
        def one(tg, carry):
            blocks = []
            for d in range(first, first + count):
                s = high * GROUP + sender(d)
                ids = jnp.where(lane < EDGE, irows[0, s], irows[1, s])
                weights = jnp.concatenate([wi[s, 0], wi[s, 1]], axis=1)
                values = x_recv_own[d].reshape(2 * EDGE, WIDTH)
                blocks.append((weights, ids, values))
            part = spread_part(tg, blocks)
            if first == 0:
                total[row_span(tg), :] = part
            else:
                total[row_span(tg), :] += part
            return carry

        lax.fori_loop(lo, hi, one, 0)

    def unit_block(u):
        return (wm[u], lanes_m[...], x_recv[u][...].reshape(2 * EDGE, WIDTH))

    def mirror_x(us, lo, hi):
        for u in us:
            x_wait(u)

        def one(tg, carry):
            blocks = [unit_block(u) for u in us]
            total[row_span(tg), :] += spread_part(tg, blocks)
            return carry

        lax.fori_loop(lo, hi, one, 0)

    def add_cut():
        def one(t, carry):
            k = (t + TILES - crows[0, 0]) % TILES
            q = cslot[0, k]
            group = jnp.where(q // GROUP == low, 0, 1)
            block = z_recv[group, (z + GROUP - q % GROUP) % GROUP]
            at = pl.ds(pl.multiple_of(t * EDGE, EDGE), EDGE)
            total[at, :] += jnp.dot(
                wc[k], block.reshape(EDGE, WIDTH), preferred_element_type=F32
            )
            return carry

        lax.fori_loop(0, TILES, one, 0, unroll=4)

    def finish(u):
        x_wait(u)

        def one(tg, carry):
            at = row_span(tg)
            spread = total[at, :] + spread_part(tg, [unit_block(u)])
            factor = scale[pl.ds(tg * SPAN, SPAN)].reshape(SPAN * EDGE, EDGE)
            factor = jnp.concatenate([factor, factor], axis=1)
            rest = base[pl.ds(tg * SPAN, SPAN)].reshape(SPAN * EDGE, WIDTH)
            out[at, :] = (factor * spread + rest).astype(BF16)
            return carry

        lax.fori_loop(0, TILES // SPAN, one, 0)

    work = {
        0: [(serve_own_x,)],
        2: [(mirror_ids,), (mirror_turn, 0, 2)],
        3: [(mirror_turn, 2, 2)],
        4: [(mirror_turn, 4, 4)],
        5: [(mirror_back, 0, 4)],
        6: [(mirror_back, 4, 4)],
        7: [(intra_degree, 0, 8)],
        8: [(intra_degree, 8, 8)],
        9: [(cut_degree,)],
        10: [(set_scale, 0, 8)],
        11: [(set_scale, 8, 8)],
        14: [(x_wait, own), (own_x, 0, 4, 0, 1), (own_x, 0, 4, 1, 2)],
        15: [(own_x, 0, 4, 2, 3), (own_x, 0, 4, 3, 4)],
        16: [(own_x, 4, 4, 0, 1), (own_x, 4, 4, 1, 2)],
        17: [(own_x, 4, 4, 2, 3), (own_x, 4, 4, 3, 4)],
        18: [(mirror_x, (0, 1, 2, 3), 0, 4)],
    }
    last = [max(r for r in range(relays) if RELAYS[r][0] == u) for u in range(units)]
    for r in range(relays + LAG):
        if r < relays:
            hop1[r].wait_recv()
            hop2[r].start()
            if r == 0:
                hear_list()
            if r in last:
                z_serve(partner_parts[last.index(r)], partner_list, last.index(r))
        if r >= LAG:
            hop2[r - LAG].wait_recv()
            if r - LAG in last:
                u = last.index(r - LAG)
                x_serve(mirror_parts[u], other_blk, u)
        for piece, *given in work.get(r, []):
            piece(*given)
    mirror_x((4, 5), 0, 4)
    z_wait(own)
    for u in range(units):
        z_wait(u)
    add_cut()
    mirror_x((6,), 0, 4)
    finish(7)

    all_asks().wait_send()
    tell.wait_send()
    sent_z = x_stage_own.at[others]
    sent_x = base.at[pl.ds(0, 2 * GROUP - 2)]
    remote(sent_z, sent_z, z_send, z_got.at[0], z_peer(1)).wait_send()
    remote(sent_x, sent_x, x_send, x_got.at[0], row_peer(1)).wait_send()
    remote(labels, panel, hop1_send, hop1_recv.at[0], partner).wait_send()
    remote(panel, panel, hop2_send, hop2_recv.at[0], beyond).wait_send()


def on_device(
    labels,
    tags,
    seed_mask,
    intra_tiles,
    intra_rows,
    intra_cols,
    send_list,
    cut_tiles,
    cut_slot,
    cut_rows,
):
    units = UNITS
    relays = len(RELAYS)

    def flat(ids):
        return jnp.swapaxes(ids[0], 0, 1)

    operands = (
        labels.reshape(TILES, PARTS, GRAIN, WIDTH),
        tags.reshape(TILES, EDGE, WIDTH),
        seed_mask.reshape(TILES, EDGE),
        intra_tiles.reshape(TILES, 2, EDGE, EDGE),
        cut_tiles.reshape(TILES, EDGE, EDGE),
        flat(intra_rows),
        flat(intra_cols),
        flat(send_list),
        cut_slot,
        cut_rows,
    )
    operands = [pltpu.with_memory_space_constraint(x, pltpu.HBM) for x in operands]
    vmem = pltpu.VMEM
    smem = pltpu.SMEM
    dma = pltpu.SemaphoreType.DMA

    def per_unit(*shape):
        return [vmem((*shape, GRAIN, WIDTH), BF16) for _ in range(UNITS)]

    scratch = [
        vmem((TILES, PARTS, GRAIN, WIDTH), BF16),
        vmem((TILES, EDGE, WIDTH), BF16),
        vmem((TILES, EDGE), I32),
        vmem((TILES, 2, EDGE, EDGE), BF16),
        vmem((TILES, EDGE, EDGE), BF16),
        smem((2, TILES), I32),
        smem((2, TILES), I32),
        smem((1, TILES), I32),
        smem((1, TILES), I32),
        smem((1, TILES), I32),
        vmem((2, TILES), I32),
        vmem((1, TILES), I32),
        vmem((GROUP, 2, TILES), I32),
        vmem((1, TILES), I32),
        smem((GROUP, 2, TILES), I32),
        smem((1, TILES), I32),
        per_unit(TILES),
        per_unit(TILES),
        vmem((GROUP, 2, PARTS, GRAIN, WIDTH), BF16),
        vmem((GROUP, 2, PARTS, GRAIN, WIDTH), BF16),
        per_unit(GROUP, 2),
        per_unit(GROUP, 2),
        vmem((GROUP, PARTS, GRAIN, WIDTH), BF16),
        per_unit(GROUP),
        vmem((2, GROUP, PARTS, GRAIN, WIDTH), BF16),
        vmem((PARTS, 2 * EDGE, EDGE), BF16),
        vmem((PARTS, EDGE, 2 * EDGE), BF16),
        vmem((GRAIN, 2 * EDGE), I32),
        vmem((EDGE, TILES), F32),
        vmem((TILES, EDGE, EDGE), F32),
        vmem((TILES, EDGE, WIDTH), F32),
        vmem((TILES * EDGE, WIDTH), F32),
        dma((12,)),
        dma,
        dma,
        dma,
        dma,
        dma,
        dma((relays,)),
        dma,
        dma((relays,)),
        dma,
        dma((units + 1,)),
        dma,
        dma((units + 1,)),
    ]
    return pl.pallas_call(
        kernel,
        out_shape=pltpu.VMEM((TILES * EDGE, WIDTH), BF16),
        in_specs=[pl.BlockSpec(memory_space=pl.ANY)] * len(operands),
        out_specs=pl.BlockSpec(memory_space=pltpu.VMEM),
        scratch_shapes=scratch,
        compiler_params=pltpu.CompilerParams(
            collective_id=0, has_side_effects=True, vmem_limit_bytes=40 * 2**20
        ),
        name="propagate",
    )(*operands)


def solution(mesh):
    both = ("dom", "blk")
    placed = (
        P(both, None),
        P(both, None),
        P(both),
        P(both, None, None, None, None),
        P(both, None, None),
        P(both, None, None),
        P(both, None, None),
        P(both, None, None, None),
        P(both, None),
        P(both, None),
    )
    return jax.shard_map(
        on_device, mesh=mesh, in_specs=placed, out_specs=P(both, None), check_vma=False
    )
```
